256 devices in a mesh: pipe: 8 (over y, z_hi), ep: 32 (over x, z_lo, core).
Axes of the slice: x: 4, y: 4, z: 8 (z_hi: 2, z_lo: 4; z = z_hi * 4 + z_lo), core: 2. Of those that a mesh axis runs over, the one named last changes fastest.
Arguments:
- first_acts: bfloat16 [8, 4096, 4096], P('pipe', 'ep'), may hold values from -6 to 6
- first_routes: int32 [8, 4096, 1], P('pipe', 'ep'), may hold values from 0 to 7; in each aligned block of 128 rows (0 to 127, 128 to 255, ..., all dimensions but the last counted through in order) at most 18 rows name the same one
- first_probs: float32 [8, 4096, 1], P('pipe', 'ep'), may hold values from 0.2 to 2
- second_acts: bfloat16 [8, 4096, 4096], P('pipe', 'ep'), may hold values from -6 to 6
- second_grads: bfloat16 [8, 4096, 4096], P('pipe', 'ep'), may hold values from -6 to 6
- second_routes: int32 [8, 4096, 1], P('pipe', 'ep'), may hold values from 0 to 7; in each aligned block of 128 rows (0 to 127, 128 to 255, ..., all dimensions but the last counted through in order) at most 18 rows name the same one
- second_probs: float32 [8, 4096, 1], P('pipe', 'ep'), may hold values from 0.2 to 2
- gate_weight: bfloat16 [8, 4096, 6144], P('pipe', None, 'ep'), may hold values from -0.09375 to 0.09375
- up_weight: bfloat16 [8, 4096, 6144], P('pipe', None, 'ep'), may hold values from -0.09375 to 0.09375
- down_weight: bfloat16 [8, 6144, 4096], P('pipe', 'ep'), may hold values from -0.21875 to 0.21875
Outputs:
- first_out: bfloat16 [8, 4096, 4096], P('pipe', 'ep')
- input_grads: bfloat16 [8, 4096, 4096], P('pipe', 'ep')
The draws below stay inside these ranges and needn't reach their ends.
Inputs may be any that keep to these rules, and one draw needn't show every extreme that they name: `first_routes`: within each aligned block of 128 tokens (the tokens of one device) no expert is named more than 18 times, and in every draw some block names some expert exactly 18 times. `second_routes`: as for first_routes.
All inputs are finite; a program needn't handle non-finite values.
Results may differ from the reference program's by a relative error of at most 0.0064.
Values may be sent and summed in bfloat16 or wider, within the bound.
A program may use at most 128 MiB of HBM per device.

```python
import math
import jax
import jax.numpy as jnp
import numpy as np
from jax import lax

D = 4096
SPLIT = 4
FF_DEV = 192
TOPK = 1
TOK_DEV = 128
FF = 768
EXPERTS = 8
CAP = 18
TOKENS = 4096
SECTIONS = 8
N_EP = 32


def shard_levels(own_key, extent, cuts, low, largest):
    factor_of, own = 1.0, jax.random.fold_in(own_key, 6)
    for dim, blocks in cuts:
        draws = jnp.exp(jax.random.uniform(jax.random.fold_in(own, dim), (blocks,), jnp.float32, low / len(cuts), largest / len(cuts)))
        factor_of = factor_of * jnp.repeat(draws, extent[dim] // blocks).reshape([-1 if axis == dim else 1 for axis in range(len(extent))])
    return factor_of


def routed_block(rng, own, number, rows, amount, top, reach, lean):
    ranking = jax.random.permutation(rng, amount)
    crowded, ordinary = load_shares(amount, rows * top, reach, lean, True), load_shares(amount, rows * top, reach, lean, False)
    places = jnp.arange(amount)

    def named(lengths, offset_by):
        used = int((lengths > 0).sum())
        fixed = max(1, used // 4)
        passed = fixed + (places - fixed + offset_by * (used - fixed)) % max(1, amount - fixed)
        return jnp.zeros((amount,), jnp.int32).at[ranking[jnp.where(places < fixed, places, passed)]].set(jnp.asarray(lengths, jnp.int32))

    lengths = jnp.where(number % 4 == 0, named(crowded, number // 4), named(ordinary, number - number // 4 - 1))
    mixed = jax.random.permutation(jax.random.fold_in(own, 3), amount)
    source_of, receiver = mixed[0:amount // 2 * 2:2], mixed[1:amount // 2 * 2:2]
    room = jnp.minimum(lengths[source_of] - 1, reach - lengths[receiver]) // 2
    room = jnp.where((source_of == ranking[0]) | (receiver == ranking[0]) | (lengths[receiver] == 0), 0, jnp.maximum(room, 0))
    passed = jax.random.randint(jax.random.fold_in(own, 4), (amount // 2,), 0, 1 << 20) % (room + 1)
    lengths = lengths.at[source_of].add(-passed).at[receiver].add(passed)
    items = jnp.searchsorted(jnp.cumsum(lengths), jnp.arange(rows * top), side="right").astype(jnp.int32)
    grid = items.reshape(top, rows).T
    grid = grid[jax.random.permutation(jax.random.fold_in(own, 1), rows)]
    offset_by = jax.random.randint(jax.random.fold_in(own, 2), (rows, 1), 0, top)
    return jnp.take_along_axis(grid, (jnp.arange(top)[None, :] + offset_by) % top, axis=1)


def load_shares(count, total, limit, skew, full):
    loads = [(1 << 20) // math.isqrt(grade ** skew) + 1 for grade in range(1, count + 1)]
    largest = limit if full else min(limit, max(-(-total // count), total * loads[0] // sum(loads)))
    least = 1 if total - largest >= count - 1 else 0
    given, spare = [largest] + [least] * (count - 1), total - largest - least * (count - 1)
    while spare > 0:
        candidates = [i for i in range(1, count) if given[i] < largest] or [i for i in range(1, count) if given[i] < limit]
        pool, budget = sum([loads[i] for i in candidates]), spare
        for i in candidates:
            addition = min(limit - given[i], max(1, budget * loads[i] // pool), spare)
            given[i] = given[i] + addition
            spare = spare - addition
    return np.array(given)


def scatter_about(key, extent, scale, reach, split=(), held_as=jnp.bfloat16):
    factor_of = shard_levels(key, extent, split, -0.22, 0.18) if split else 1.0
    array = jax.random.normal(key, extent, jnp.float32) * scale * factor_of
    return jnp.minimum(jnp.maximum(array, -reach), reach).astype(held_as)


def setup_inputs(seed: int = 0) -> dict:
    streams_of = jax.random.split(jax.random.key(seed), 11)
    first_acts = scatter_about(streams_of[0], (SECTIONS, TOKENS, D), 1.0, 6.0, ((0, 8), (1, 32)))
    first_routes_keys = jax.random.split(jax.random.fold_in(streams_of[1], 1), SECTIONS * TOKENS // TOK_DEV)
    first_routes_turns = jax.random.permutation(jax.random.fold_in(streams_of[1], 3), SECTIONS * TOKENS // TOK_DEV)
    first_routes = jax.vmap(lambda own, number: routed_block(jax.random.fold_in(streams_of[1], 2), own, number, TOK_DEV, EXPERTS, TOPK, CAP, 1))(first_routes_keys, first_routes_turns).reshape((SECTIONS, TOKENS, TOPK))
    first_probs = jnp.clip(jnp.exp(math.log(2.0) - 2.3025851 * jax.random.uniform(streams_of[2], (SECTIONS, TOKENS, TOPK), jnp.float32) ** shard_levels(streams_of[2], (SECTIONS, TOKENS, TOPK), ((0, 8), (1, 32)), -0.2, 0.2)), 0.2, 2.0)
    second_acts = scatter_about(streams_of[3], (SECTIONS, TOKENS, D), 1.0, 6.0, ((0, 8), (1, 32)))
    second_grads = scatter_about(streams_of[4], (SECTIONS, TOKENS, D), 1.0, 6.0, ((0, 8), (1, 32)))
    second_routes_keys = jax.random.split(jax.random.fold_in(streams_of[5], 1), SECTIONS * TOKENS // TOK_DEV)
    second_routes_turns = jax.random.permutation(jax.random.fold_in(streams_of[5], 3), SECTIONS * TOKENS // TOK_DEV)
    second_routes = jax.vmap(lambda own, number: routed_block(jax.random.fold_in(streams_of[5], 2), own, number, TOK_DEV, EXPERTS, TOPK, CAP, 1))(second_routes_keys, second_routes_turns).reshape((SECTIONS, TOKENS, TOPK))
    second_probs = jnp.clip(jnp.exp(math.log(2.0) - 2.3025851 * jax.random.uniform(streams_of[6], (SECTIONS, TOKENS, TOPK), jnp.float32) ** shard_levels(streams_of[6], (SECTIONS, TOKENS, TOPK), ((0, 8), (1, 32)), -0.2, 0.2)), 0.2, 2.0)
    gate_weight = scatter_about(streams_of[7], (SECTIONS, D, EXPERTS * FF), D ** -0.5, 0.09375, ((0, 8), (2, 32)))
    up_weight = scatter_about(streams_of[8], (SECTIONS, D, EXPERTS * FF), D ** -0.5, 0.09375, ((0, 8), (2, 32)))
    down_weight = scatter_about(streams_of[9], (SECTIONS, EXPERTS * FF, D), FF ** -0.5, 0.21875, ((0, 8), (1, 32)))
    return dict(first_acts=first_acts, first_routes=first_routes, first_probs=first_probs, second_acts=second_acts, second_grads=second_grads, second_routes=second_routes, second_probs=second_probs, gate_weight=gate_weight, up_weight=up_weight, down_weight=down_weight)


def expert_forward(rows, gate_part, up_part, down_part):
    gate = jnp.dot(rows, gate_part, preferred_element_type=jnp.float32)
    upper = jnp.dot(rows, up_part, preferred_element_type=jnp.float32)
    hidden = (jax.nn.silu(gate) * upper).astype(jnp.bfloat16)
    return jnp.dot(hidden, down_part, preferred_element_type=jnp.float32).astype(jnp.bfloat16)


def expert_backward(rows, grads, gate_part, up_part, down_part):
    gate = jnp.dot(rows, gate_part, preferred_element_type=jnp.float32)
    upper = jnp.dot(rows, up_part, preferred_element_type=jnp.float32)
    d_hidden = jnp.dot(grads, down_part.T, preferred_element_type=jnp.float32)
    sig = jax.nn.sigmoid(gate)
    d_gate = (d_hidden * upper * sig * (1.0 + gate * (1.0 - sig))).astype(jnp.bfloat16)
    d_up = (d_hidden * gate * sig).astype(jnp.bfloat16)
    total = jnp.dot(d_gate, gate_part.T, preferred_element_type=jnp.float32)
    total = total + jnp.dot(d_up, up_part.T, preferred_element_type=jnp.float32)
    return total.astype(jnp.bfloat16)


def positions(routes):
    expert = routes[:, 0].astype(jnp.int32)
    onehot = (expert[:, None] == jnp.arange(EXPERTS, dtype=jnp.int32)[None, :]).astype(jnp.int32)
    blocks = onehot.reshape(N_EP, TOK_DEV, EXPERTS)
    before = jnp.cumsum(blocks, axis=1) - blocks
    slot = jnp.sum(before * blocks, axis=2).reshape(TOKENS)
    device = jnp.arange(TOKENS, dtype=jnp.int32) // TOK_DEV
    return ((expert * N_EP + device) * CAP + slot).astype(jnp.int32)


def place(values, where):
    empty = jnp.zeros((EXPERTS * N_EP * CAP, D), values.dtype)
    return empty.at[where].set(values).reshape(EXPERTS, N_EP * CAP, D)


def section_forward(inputs, where, gate_w, up_w, down_w):
    buffer = place(inputs, where)
    gates = gate_w.reshape(D, EXPERTS, SPLIT, FF_DEV).transpose(1, 2, 0, 3)
    ups = up_w.reshape(D, EXPERTS, SPLIT, FF_DEV).transpose(1, 2, 0, 3)
    downs = down_w.reshape(EXPERTS, SPLIT, FF_DEV, D)

    def one_expert(args):
        rows, gate_e, up_e, down_e = args
        total = jnp.zeros((N_EP * CAP, D), jnp.float32)
        for block in range(SPLIT):
            total = total + expert_forward(rows, gate_e[block], up_e[block], down_e[block]).astype(jnp.float32)
        return total

    sums = lax.map(one_expert, (buffer, gates, ups, downs))
    return sums.reshape(EXPERTS * N_EP * CAP, D)[where]


def section_backward(inputs, scaled, where, gate_w, up_w, down_w):
    buffer = place(inputs, where)
    grads = place(scaled, where)
    gates = gate_w.reshape(D, EXPERTS, SPLIT, FF_DEV).transpose(1, 2, 0, 3)
    ups = up_w.reshape(D, EXPERTS, SPLIT, FF_DEV).transpose(1, 2, 0, 3)
    downs = down_w.reshape(EXPERTS, SPLIT, FF_DEV, D)

    def one_expert(args):
        rows, grad_rows, gate_e, up_e, down_e = args
        total = jnp.zeros((N_EP * CAP, D), jnp.float32)
        for block in range(SPLIT):
            total = total + expert_backward(rows, grad_rows, gate_e[block], up_e[block], down_e[block]).astype(jnp.float32)
        return total

    sums = lax.map(one_expert, (buffer, grads, gates, ups, downs))
    return sums.reshape(EXPERTS * N_EP * CAP, D)[where]


def reference(first_acts, first_routes, first_probs, second_acts, second_grads, second_routes, second_probs, gate_weight, up_weight, down_weight):
    arrived = jnp.roll(first_acts, 1, axis=0)
    returned = jnp.roll(second_grads, -1, axis=0)
    outs = []
    grads_out = []
    for section in range(SECTIONS):
        where = positions(first_routes[section])
        summed = section_forward(arrived[section], where, gate_weight[section], up_weight[section], down_weight[section])
        outs.append((first_probs[section] * summed).astype(jnp.bfloat16))
        where_two = positions(second_routes[section])
        scaled = (second_probs[section] * returned[section].astype(jnp.float32)).astype(jnp.bfloat16)
        back = section_backward(second_acts[section], scaled, where_two, gate_weight[section], up_weight[section], down_weight[section])
        grads_out.append(back.astype(jnp.bfloat16))
    return jnp.stack(outs), jnp.stack(grads_out)
```

```python
import jax
import jax.numpy as jnp
from jax import lax
from jax.experimental import pallas as pl
from jax.experimental.pallas import tpu as pltpu
from jax.sharding import PartitionSpec as P

MESH = pl.DeviceIdType.MESH
F32 = jnp.float32
BF16 = jnp.bfloat16
NT = (((1,), (1,)), ((), ()))

TOK = 128
D = 4096
HID = 192
EXPERTS = 8
KB = 512
NK = D // KB
W = D + KB
BLK = 16
SRC = 32
MAIN = SRC * BLK
EXTRA = SRC * 2
ROWS = MAIN + EXTRA
SECTIONS = 8

ONE, ACTS, GRADS = 0, 1, 2


def rows16(index):
    return pl.ds(pl.multiple_of(index * BLK, BLK), BLK)


def cols(index):
    return pl.ds(pl.multiple_of(index * KB, KB), KB)


def iota(shape, dim):
    return lax.broadcasted_iota(jnp.int32, shape, dim)


def onehot(mask):
    return jnp.where(mask, 1.0, 0.0).astype(BF16)


def codes(expert_col):
    here, there = iota((TOK, TOK), 0), iota((TOK, TOK), 1)
    col = jnp.broadcast_to(expert_col.astype(F32), (TOK, TOK))
    row = jnp.sum(jnp.where(here == there, col, 0.0), axis=0, keepdims=True)
    same = jnp.where(col == row, 1.0, 0.0)
    slot_col = jnp.sum(jnp.where(there < here, same, 0.0), axis=1, keepdims=True)
    slot_row = jnp.sum(jnp.where(here < there, same, 0.0), axis=0, keepdims=True)

    def both(expert, slot):
        main = jnp.where(slot < BLK, expert * BLK + slot, -1.0)
        tail = jnp.where(slot < BLK, -1024.0, expert * BLK + slot - BLK)
        return main, tail

    return both(col[:, 0:1], slot_col), both(row, slot_row)


def entry_own(z, q):
    return jnp.where(q == 0, jnp.minimum(z, 1), jnp.maximum(z, 2))


def entry_far(z, q):
    return jnp.where(q == 0, jnp.where(z == 0, 1, 0), jnp.where(z == 3, 2, 3))


def kernel(
    routes_one, probs_one, routes_two, probs_two, one_hbm, acts_hbm, grads_hbm, gate_hbm, up_hbm, down_hbm,
    out_one, out_two,
    held, wg, wu, wd, meta_out, meta_in, stage, recv, part, cx, px, home, acc, hid,
    load_sem, msend, mrecv, dsend, fsend, csend, rsem, xsend, xrecv, psend, precv, hsend, hrecv,
):
    p, j = lax.axis_index("pipe"), lax.axis_index("ep")
    x, z, c = j // 8, (j // 2) % 4, j % 2
    q = z // 2
    expert = j // 4
    mine = c * 16 + x * 4 + z
    other = x * 8 + z * 2 + (1 - c)
    pair = x * 8 + (q * 4 + 1 - z) * 2 + c
    after, before = lax.rem(p + 1, SECTIONS), lax.rem(p + SECTIONS - 1, SECTIONS)
    section = {ONE: after, ACTS: p, GRADS: before}

    def entry(d, source_z, pair_index):
        return entry_own(source_z, pair_index) if d == ACTS else entry_far(source_z, pair_index)

    loads = [
        pltpu.make_async_copy(src, dst, load_sem.at[i])
        for i, (src, dst) in enumerate(
            [
                (acts_hbm, held.at[ACTS]),
                (one_hbm, held.at[ONE]),
                (grads_hbm, held.at[GRADS]),
                (gate_hbm, wg),
                (up_hbm, wu),
                (down_hbm, wd),
            ]
        )
    ]
    for load in loads:
        load.start()

    barrier = pltpu.get_barrier_semaphore()

    def greet(n, carry):
        them = (n // 4) * 8 + (n % 4) * 2 + c
        pl.semaphore_signal(barrier, inc=1, device_id=(after, them), device_id_type=MESH)
        pl.semaphore_signal(barrier, inc=1, device_id=(before, them), device_id_type=MESH)

        @pl.when(them != j)
        def _():
            pl.semaphore_signal(barrier, inc=1, device_id=(p, them), device_id_type=MESH)

        return carry

    lax.fori_loop(0, 16, greet, 0)
    pl.semaphore_signal(barrier, inc=1, device_id=(p, other), device_id_type=MESH)

    (main_col_one, tail_col_one), (main_row_one, tail_row_one) = codes(routes_one[...])
    (main_col_two, tail_col_two), (main_row_two, tail_row_two) = codes(routes_two[...])
    eye = iota((TOK, TOK), 0) == iota((TOK, TOK), 1)
    prob_row_two = jnp.sum(jnp.where(eye, jnp.broadcast_to(probs_two[...], (TOK, TOK)), 0.0), axis=0, keepdims=True)
    meta_out[0, 0:1, :] = main_row_one
    meta_out[0, 1:2, :] = tail_row_one
    meta_out[0, 2:8, :] = jnp.zeros((6, TOK), F32)
    meta_out[1, 0:1, :] = main_row_two
    meta_out[1, 1:2, :] = tail_row_two
    meta_out[1, 2:3, :] = prob_row_two
    meta_out[1, 3:8, :] = jnp.zeros((5, TOK), F32)

    pl.semaphore_wait(barrier, 48)

    metas = [
        pltpu.make_async_remote_copy(
            meta_out.at[i], meta_in.at[i], msend.at[i], mrecv.at[i], device_id=(to, j), device_id_type=MESH
        )
        for i, to in enumerate((before, after))
    ]
    for copy in metas:
        copy.start()

    def fill(d, main_row, tail_row, prob_row):
        row = iota((TOK, TOK), 0).astype(F32)
        here = row == main_row
        table = onehot(here)
        tail = jnp.zeros((TOK, KB), F32)
        tail_prob = jnp.zeros((TOK, 1), F32)
        if prob_row is not None:
            prob = jnp.sum(jnp.where(here, prob_row, 0.0), axis=1, keepdims=True)
        for k in range(NK):
            values = held[d, :, k * KB : (k + 1) * KB]
            got = jnp.dot(table, values, preferred_element_type=F32)
            there = row == tail_row + 2.0 * k
            tail = tail + jnp.dot(onehot(there), values, preferred_element_type=F32)
            if prob_row is not None:
                got = prob * got
                tail_prob = tail_prob + jnp.sum(jnp.where(there, prob_row, 0.0), axis=1, keepdims=True)
            stage[d, :, k * KB : (k + 1) * KB] = got.astype(BF16)
        if prob_row is not None:
            tail = tail_prob * tail
        stage[d, :, D:W] = tail.astype(BF16)

    def dispatch(d, e):
        target = (e // 2) * 8 + entry(d, z, e % 2) * 2 + c
        return target, pltpu.make_async_remote_copy(
            stage.at[d, rows16(e)],
            recv.at[d, rows16(mine)],
            dsend.at[d, e],
            rsem.at[d, mine],
            device_id=(section[d], target),
            device_id_type=MESH,
        )

    def send_all(d):
        def step(n, carry):
            e = lax.rem(x * 2 + n, EXPERTS)
            target, copy = dispatch(d, e)
            if d == ACTS:
                pl.when(target != j)(copy.start)

                @pl.when(target == j)
                def _():
                    pltpu.make_async_copy(stage.at[d, rows16(e)], recv.at[d, rows16(mine)], rsem.at[d, mine]).start()
            else:
                copy.start()
            return carry

        lax.fori_loop(0, EXPERTS, step, 0)

    def arrived(d, b):
        pltpu.make_async_copy(recv.at[d, rows16(b)], recv.at[d, rows16(b)], rsem.at[d, b]).wait()

    def onward(d, n, to, sem):
        b = c * 16 + n
        return pltpu.make_async_remote_copy(
            recv.at[d, rows16(b)],
            recv.at[d, rows16(b)],
            sem.at[d, n],
            rsem.at[d, b],
            device_id=(p, to),
            device_id_type=MESH,
        )

    def forward(d, direct):
        def step(n, carry):
            enters = entry(d, n % 4, q) == z

            @pl.when(enters if direct else jnp.logical_not(enters))
            def _():
                arrived(d, c * 16 + n)
                if direct:
                    onward(d, n, pair, fsend).start()
                onward(d, n, other, csend).start()

            return carry

        lax.fori_loop(0, 16, step, 0)

    def from_core(d):
        def step(n, carry):
            arrived(d, (1 - c) * 16 + n)
            return carry

        lax.fori_loop(0, 16, step, 0)

    def unfold(d):
        row, col = iota((EXTRA, MAIN), 0), iota((EXTRA, MAIN), 1)
        base = (row // 2) * BLK + row % 2
        tail = recv[d, 0:MAIN, D:W]
        for k in range(NK):
            pick = onehot(col == base + 2 * k)
            recv[d, MAIN:ROWS, k * KB : (k + 1) * KB] = jnp.dot(pick, tail, preferred_element_type=F32).astype(BF16)

    def fold(m):
        row, col = iota((MAIN, EXTRA), 0), iota((MAIN, EXTRA), 1)
        base = (col // 2) * BLK + col % 2
        tail = jnp.zeros((MAIN, KB), F32)
        for k in range(NK):
            pick = onehot(row == base + 2 * k)
            tail = tail + jnp.dot(pick, part[m, MAIN:ROWS, k * KB : (k + 1) * KB], preferred_element_type=F32)
        part[m, 0:MAIN, D:W] = tail.astype(BF16)

    def gate_up(d):
        acc[0:2] = jnp.zeros((2, ROWS, HID), F32)

        def step(k, carry):
            values = recv[d, :, cols(k)]
            acc[0] += jnp.dot(values, wg[cols(k), :], preferred_element_type=F32)
            acc[1] += jnp.dot(values, wu[cols(k), :], preferred_element_type=F32)
            return carry

        lax.fori_loop(0, NK, step, 0)

    def forward_compute():
        unfold(ONE)
        gate_up(ONE)
        gate = acc[0]
        hid[0] = (gate * jax.nn.sigmoid(gate) * acc[1]).astype(BF16)

        def step(k, carry):
            part[0, :, cols(k)] = jnp.dot(hid[0], wd[:, cols(k)], preferred_element_type=F32).astype(BF16)
            return carry

        lax.fori_loop(0, NK, step, 0)
        fold(0)

    def backward_compute():
        unfold(GRADS)
        acc[2] = jnp.zeros((ROWS, HID), F32)

        def down(k, carry):
            acc[2] += lax.dot_general(recv[GRADS, :, cols(k)], wd[:, cols(k)], NT, preferred_element_type=F32)
            return carry

        lax.fori_loop(0, NK, down, 0)
        gate = acc[0]
        sig = jax.nn.sigmoid(gate)
        slope = acc[2] * sig
        hid[0] = (slope * acc[1] * (1.0 + gate * (1.0 - sig))).astype(BF16)
        hid[1] = (slope * gate).astype(BF16)

        def step(k, carry):
            total = lax.dot_general(hid[0], wg[cols(k), :], NT, preferred_element_type=F32)
            total = total + lax.dot_general(hid[1], wu[cols(k), :], NT, preferred_element_type=F32)
            part[1, :, cols(k)] = total.astype(BF16)
            return carry

        lax.fori_loop(0, NK, step, 0)
        fold(1)

    def to_core(m, g):
        quarter = pl.ds(pl.multiple_of((1 - c) * 256 + g * 64, 64), 64)
        return pltpu.make_async_remote_copy(
            part.at[m, quarter],
            cx.at[m, pl.ds(g * 64, 64)],
            xsend.at[m, g],
            xrecv.at[m, g],
            device_id=(p, other),
            device_id_type=MESH,
        )

    def add_into(m, n, ref):
        b = rows16(c * 16 + n)
        part[m, b, :] = (part[m, b, :].astype(F32) + ref[m, rows16(n), :].astype(F32)).astype(BF16)

    def to_pair(m, n):
        return pltpu.make_async_remote_copy(
            part.at[m, rows16(c * 16 + n)],
            px.at[m, rows16(n)],
            psend.at[m, n],
            precv.at[m, n],
            device_id=(p, pair),
            device_id_type=MESH,
        )

    def to_home(m, n):
        target = (n // 4) * 8 + (n % 4) * 2 + c
        return target, pltpu.make_async_remote_copy(
            part.at[m, rows16(c * 16 + n)],
            home.at[m, rows16(expert)],
            hsend.at[m, n],
            hrecv.at[m, expert],
            device_id=(p, target),
            device_id_type=MESH,
        )

    def leaves_here(n):
        return entry_own(n % 4, q) == z

    def return_first(m):
        for g in range(4):
            pltpu.make_async_copy(cx.at[m, pl.ds(g * 64, 64)], cx.at[m, pl.ds(g * 64, 64)], xrecv.at[m, g]).wait()

            def step(n, carry):
                add_into(m, n, cx)

                @pl.when(jnp.logical_not(leaves_here(n)))
                def _():
                    to_pair(m, n).start()

                return carry

            lax.fori_loop(g * 4, g * 4 + 4, step, 0)

    def return_second(m):
        def step(n, carry):
            @pl.when(leaves_here(n))
            def _():
                pltpu.make_async_copy(px.at[m, rows16(n)], px.at[m, rows16(n)], precv.at[m, n]).wait()
                add_into(m, n, px)
                target, copy = to_home(m, n)
                pl.when(target != j)(copy.start)

                @pl.when(target == j)
                def _():
                    pltpu.make_async_copy(
                        part.at[m, rows16(c * 16 + n)], home.at[m, rows16(expert)], hrecv.at[m, expert]
                    ).start()

            return carry

        lax.fori_loop(0, 16, step, 0)

    def collect(m, main_col, tail_col, prob_col, out):
        def step(e, carry):
            pltpu.make_async_copy(home.at[m, rows16(e)], home.at[m, rows16(e)], hrecv.at[m, e]).wait()
            return carry

        lax.fori_loop(0, EXPERTS, step, 0)
        row = iota((TOK, TOK), 1).astype(F32)
        table = onehot(row == main_col)
        tail = home[m, :, D:W]
        for k in range(NK):
            got = jnp.dot(table, home[m, :, k * KB : (k + 1) * KB], preferred_element_type=F32)
            got = got + jnp.dot(onehot(row == tail_col + 2.0 * k), tail, preferred_element_type=F32)
            if prob_col is not None:
                got = prob_col * got
            out[:, k * KB : (k + 1) * KB] = got.astype(BF16)

    loads[0].wait()
    fill(ACTS, main_row_two, tail_row_two, None)
    send_all(ACTS)
    loads[1].wait()
    metas[0].wait_recv()
    fill(ONE, meta_in[0, 0:1, :], meta_in[0, 1:2, :], None)
    send_all(ONE)
    loads[2].wait()
    metas[1].wait_recv()
    fill(GRADS, meta_in[1, 0:1, :], meta_in[1, 1:2, :], meta_in[1, 2:3, :])
    send_all(GRADS)

    forward(ACTS, True)
    forward(ONE, True)
    forward(ACTS, False)
    forward(ONE, False)
    from_core(ONE)
    for load in loads[3:]:
        load.wait()
    forward_compute()
    for g in range(4):
        to_core(0, g).start()
    from_core(ACTS)
    unfold(ACTS)
    gate_up(ACTS)
    return_first(0)
    forward(GRADS, True)
    return_second(0)
    forward(GRADS, False)
    from_core(GRADS)
    backward_compute()
    for g in range(4):
        to_core(1, g).start()
    collect(0, main_col_one, tail_col_one, probs_one[...], out_one)
    return_first(1)
    return_second(1)
    collect(1, main_col_two, tail_col_two, None, out_two)

    for copy in metas:
        copy.wait_send()

    for d in (ACTS, ONE, GRADS):

        def sent(e, carry):
            target, copy = dispatch(d, e)
            if d == ACTS:
                pl.when(target != j)(copy.wait_send)
            else:
                copy.wait_send()
            return carry

        lax.fori_loop(0, EXPERTS, sent, 0)

        def passed(n, carry):
            @pl.when(entry(d, n % 4, q) == z)
            def _():
                onward(d, n, pair, fsend).wait_send()

            onward(d, n, other, csend).wait_send()
            return carry

        lax.fori_loop(0, 16, passed, 0)

    for m in range(2):
        for g in range(4):
            to_core(m, g).wait_send()

        def returned(n, carry):
            leaves = leaves_here(n)

            @pl.when(jnp.logical_not(leaves))
            def _():
                to_pair(m, n).wait_send()

            target, copy = to_home(m, n)
            pl.when(jnp.logical_and(leaves, target != j))(copy.wait_send)
            return carry

        lax.fori_loop(0, 16, returned, 0)


def body(
    first_acts,
    first_routes,
    first_probs,
    second_acts,
    second_grads,
    second_routes,
    second_probs,
    gate_weight,
    up_weight,
    down_weight,
):
    vmem = pl.BlockSpec(memory_space=pltpu.VMEM)
    hbm = pl.BlockSpec(memory_space=pl.ANY)
    dma = pltpu.SemaphoreType.DMA
    result = jax.ShapeDtypeStruct((TOK, D), BF16)
    first_out, input_grads = pl.pallas_call(
        kernel,
        out_shape=(result, result),
        in_specs=[vmem] * 4 + [hbm] * 6,
        out_specs=(vmem, vmem),
        scratch_shapes=[
            pltpu.VMEM((3, TOK, D), BF16),
            pltpu.VMEM((D, HID), BF16),
            pltpu.VMEM((D, HID), BF16),
            pltpu.VMEM((HID, D), BF16),
            pltpu.VMEM((2, 8, TOK), F32),
            pltpu.VMEM((2, 8, TOK), F32),
            pltpu.VMEM((3, EXPERTS * BLK, W), BF16),
            pltpu.VMEM((3, ROWS, W), BF16),
            pltpu.VMEM((2, ROWS, W), BF16),
            pltpu.VMEM((2, MAIN // 2, W), BF16),
            pltpu.VMEM((2, MAIN // 2, W), BF16),
            pltpu.VMEM((2, EXPERTS * BLK, W), BF16),
            pltpu.VMEM((3, ROWS, HID), F32),
            pltpu.VMEM((2, ROWS, HID), BF16),
            dma((6,)),
            dma((2,)),
            dma((2,)),
            dma((3, EXPERTS)),
            dma((3, 16)),
            dma((3, 16)),
            dma((3, SRC)),
            dma((2, 4)),
            dma((2, 4)),
            dma((2, 16)),
            dma((2, 16)),
            dma((2, 16)),
            dma((2, EXPERTS)),
        ],
        compiler_params=pltpu.CompilerParams(
            collective_id=0, has_side_effects=True, vmem_limit_bytes=63 * 1024 * 1024
        ),
    )(
        first_routes[0],
        first_probs[0],
        second_routes[0],
        second_probs[0],
        first_acts[0],
        second_acts[0],
        second_grads[0],
        gate_weight[0],
        up_weight[0],
        down_weight[0],
    )
    return (first_out[None], input_grads[None])


def solution(mesh):
    in_specs = (
        P("pipe", "ep", None),
        P("pipe", "ep", None),
        P("pipe", "ep", None),
        P("pipe", "ep", None),
        P("pipe", "ep", None),
        P("pipe", "ep", None),
        P("pipe", "ep", None),
        P("pipe", None, "ep"),
        P("pipe", None, "ep"),
        P("pipe", "ep", None),
    )
    out_specs = (P("pipe", "ep", None), P("pipe", "ep", None))
    return jax.shard_map(body, mesh=mesh, in_specs=in_specs, out_specs=out_specs, check_vma=False)
```

```python
import jax
import jax.numpy as jnp
from jax import lax
from jax.experimental import pallas as pl
from jax.experimental.pallas import tpu as pltpu
from jax.sharding import PartitionSpec as P

MESH = pl.DeviceIdType.MESH
F32 = jnp.float32
BF16 = jnp.bfloat16
NT = (((1,), (1,)), ((), ()))

TOK = 128
D = 4096
HID = 192
EXPERTS = 8
KB = 512
NK = D // KB
W = D + KB
BLK = 16
SRC = 32
HALF = SRC // 2
MAIN = HALF * BLK
EXTRA = HALF * 2
ROWS = MAIN + EXTRA
SECTIONS = 8

ONE, ACTS, GRADS = 0, 1, 2


def rows16(index):
    return pl.ds(pl.multiple_of(index * BLK, BLK), BLK)


def cols(index):
    return pl.ds(pl.multiple_of(index * KB, KB), KB)


def iota(shape, dim):
    return lax.broadcasted_iota(jnp.int32, shape, dim)


def onehot(mask):
    return jnp.where(mask, 1.0, 0.0).astype(BF16)


def column(row):
    eye = iota((TOK, TOK), 0) == iota((TOK, TOK), 1)
    return jnp.sum(jnp.where(eye, jnp.broadcast_to(row, (TOK, TOK)), 0.0), axis=1, keepdims=True)


def codes(expert_row):
    here, there = iota((TOK, TOK), 0), iota((TOK, TOK), 1)
    row = expert_row.astype(F32)
    col = column(row)
    same = jnp.where(col == row, 1.0, 0.0)
    slot_col = jnp.sum(jnp.where(there < here, same, 0.0), axis=1, keepdims=True)
    slot_row = jnp.sum(jnp.where(here < there, same, 0.0), axis=0, keepdims=True)

    def both(expert, slot):
        main = jnp.where(slot < BLK, expert * BLK + slot, -1.0)
        tail = jnp.where(slot < BLK, -1024.0, expert * BLK + slot - BLK)
        return main, tail

    return both(col, slot_col), both(row, slot_row)


def entry_own(z, q):
    return jnp.where(q == 0, jnp.minimum(z, 1), jnp.maximum(z, 2))


def entry_far(z, q):
    return jnp.where(q == 0, jnp.where(z == 0, 1, 0), jnp.where(z == 3, 2, 3))


def kernel(
    routes_one, probs_one, routes_two, probs_two, one_hbm, acts_hbm, grads_hbm, gate_hbm, up_hbm, down_hbm,
    out_one, out_two,
    held, wg, wu, wd, meta_out, meta_in, stage, recv, part, cx, px, home, acc, hid,
    load_sem, msend, mrecv, dsend, fsend, csend, rsem, xsend, xrecv, psend, precv, hsend, hrecv,
):
    p, j = lax.axis_index("pipe"), lax.axis_index("ep")
    x, z, c = j // 8, (j // 2) % 4, j % 2
    q = z // 2
    expert = j // 4
    other = x * 8 + z * 2 + (1 - c)
    pair = x * 8 + (q * 4 + 1 - z) * 2 + c
    after, before = lax.rem(p + 1, SECTIONS), lax.rem(p + SECTIONS - 1, SECTIONS)
    section = {ONE: after, ACTS: p, GRADS: before}

    def entry(d, source_z, pair_index):
        return entry_own(source_z, pair_index) if d == ACTS else entry_far(source_z, pair_index)

    loads = [
        pltpu.make_async_copy(src, dst, load_sem.at[i])
        for i, (src, dst) in enumerate(
            [
                (acts_hbm, held.at[ACTS]),
                (one_hbm, held.at[ONE]),
                (grads_hbm, held.at[GRADS]),
                (gate_hbm, wg),
                (up_hbm, wu),
                (down_hbm, wd),
            ]
        )
    ]
    for load in loads:
        load.start()

    barrier = pltpu.get_barrier_semaphore()

    def greet(n, carry):
        them = (n // 4) * 8 + (n % 4) * 2 + c
        pl.semaphore_signal(barrier, inc=1, device_id=(after, them), device_id_type=MESH)
        pl.semaphore_signal(barrier, inc=1, device_id=(before, them), device_id_type=MESH)

        @pl.when(them != j)
        def _():
            pl.semaphore_signal(barrier, inc=1, device_id=(p, them), device_id_type=MESH)

        return carry

    lax.fori_loop(0, 16, greet, 0)
    pl.semaphore_signal(barrier, inc=1, device_id=(p, other), device_id_type=MESH)

    (main_col_one, tail_col_one), (main_row_one, tail_row_one) = codes(routes_one[...])
    (main_col_two, tail_col_two), (main_row_two, tail_row_two) = codes(routes_two[...])
    meta_out[0, 0:1, :] = main_row_one
    meta_out[0, 1:2, :] = tail_row_one
    meta_out[0, 2:8, :] = jnp.zeros((6, TOK), F32)
    meta_out[1, 0:1, :] = main_row_two
    meta_out[1, 1:2, :] = tail_row_two
    meta_out[1, 2:3, :] = probs_two[...]
    meta_out[1, 3:8, :] = jnp.zeros((5, TOK), F32)

    pl.semaphore_wait(barrier, 48)

    metas = [
        pltpu.make_async_remote_copy(
            meta_out.at[i], meta_in.at[i], msend.at[i], mrecv.at[i], device_id=(to, j), device_id_type=MESH
        )
        for i, to in enumerate((before, after))
    ]
    for copy in metas:
        copy.start()

    def fill(d, main_row, tail_row, prob_row):
        row = iota((TOK, TOK), 0).astype(F32)
        here = row == main_row
        table = onehot(here)
        tail = jnp.zeros((TOK, KB), F32)
        tail_prob = jnp.zeros((TOK, 1), F32)
        if prob_row is not None:
            prob = jnp.sum(jnp.where(here, prob_row, 0.0), axis=1, keepdims=True)
        for k in range(NK):
            values = held[d, :, k * KB : (k + 1) * KB]
            got = jnp.dot(table, values, preferred_element_type=F32)
            there = row == tail_row + 2.0 * k
            tail = tail + jnp.dot(onehot(there), values, preferred_element_type=F32)
            if prob_row is not None:
                got = prob * got
                tail_prob = tail_prob + jnp.sum(jnp.where(there, prob_row, 0.0), axis=1, keepdims=True)
            stage[d, :, k * KB : (k + 1) * KB] = got.astype(BF16)
        if prob_row is not None:
            tail = tail_prob * tail
        stage[d, :, D:W] = tail.astype(BF16)

    def place(r, core, source_z):
        return r // 2, (r % 2) * 8 + core * 4 + source_z

    def source(i):
        return i // 4, jnp.where(q == 0, 3 - i % 4, i % 4)

    def launch(move, may_stay):
        target, src, dst, send_sem, sem, device = move

        def remote():
            pltpu.make_async_remote_copy(src, dst, send_sem, sem, device_id=device, device_id_type=MESH).start()

        if not may_stay:
            remote()
            return
        pl.when(target != j)(remote)

        @pl.when(target == j)
        def _():
            pltpu.make_async_copy(src, dst, sem).start()

    def sent(move, may_stay, when=True):
        target, src, dst, send_sem, sem, device = move

        def wait():
            pltpu.make_async_remote_copy(src, dst, send_sem, sem, device_id=device, device_id_type=MESH).wait_send()

        if may_stay:
            pl.when(jnp.logical_and(when, target != j))(wait)
        else:
            wait()

    def dispatch(d, i):
        r = i // 2
        e = lax.rem(x + r, 4) * 2 + i % 2
        target = (e // 2) * 8 + entry(d, z, e % 2) * 2 + c
        h, b = place(r, c, z)
        sem = rsem.at[d, h * HALF + b]
        src, dst = stage.at[d, rows16(e)], recv.at[d, h, rows16(b)]
        return target, src, dst, dsend.at[d, i], sem, (section[d], target)

    def send(d, low, high):
        def step(i, carry):
            launch(dispatch(d, i), d == ACTS)
            return carry

        lax.fori_loop(low, high, step, 0)

    def arrived(d, h, b):
        ref = recv.at[d, h, rows16(b)]
        pltpu.make_async_copy(ref, ref, rsem.at[d, h * HALF + b]).wait()

    def onward(d, i, to, sem):
        r, source_z = source(i)
        h, b = place(r, c, source_z)
        ref = recv.at[d, h, rows16(b)]
        return pltpu.make_async_remote_copy(
            ref, ref, sem.at[d, i], rsem.at[d, h * HALF + b], device_id=(p, to), device_id_type=MESH
        )

    def forward(d, half, direct):
        def step(i, carry):
            r, source_z = source(i)
            enters = entry(d, source_z, q) == z

            @pl.when(enters if direct else jnp.logical_not(enters))
            def _():
                h, b = place(r, c, source_z)
                arrived(d, h, b)
                if direct:
                    onward(d, i, pair, fsend).start()
                onward(d, i, other, csend).start()

            return carry

        lax.fori_loop(half * 8, half * 8 + 8, step, 0)

    def from_core(d, half):
        def step(i, carry):
            r, source_z = source(i)
            h, b = place(r, 1 - c, source_z)
            arrived(d, h, b)
            return carry

        lax.fori_loop(half * 8, half * 8 + 8, step, 0)

    def unfold(d, h):
        row, col = iota((EXTRA, MAIN), 0), iota((EXTRA, MAIN), 1)
        base = (row // 2) * BLK + row % 2
        tail = recv[d, h, 0:MAIN, D:W]
        for k in range(NK):
            pick = onehot(col == base + 2 * k)
            recv[d, h, MAIN:ROWS, k * KB : (k + 1) * KB] = jnp.dot(pick, tail, preferred_element_type=F32).astype(BF16)

    def fold(m, h):
        row, col = iota((MAIN, EXTRA), 0), iota((MAIN, EXTRA), 1)
        base = (col // 2) * BLK + col % 2
        tail = jnp.zeros((MAIN, KB), F32)
        for k in range(NK):
            pick = onehot(row == base + 2 * k)
            tail = tail + jnp.dot(pick, part[m, h, MAIN:ROWS, k * KB : (k + 1) * KB], preferred_element_type=F32)
        part[m, h, 0:MAIN, D:W] = tail.astype(BF16)

    def gate_up(d, h):
        unfold(d, h)
        acc[h, 0:2] = jnp.zeros((2, ROWS, HID), F32)

        def step(k, carry):
            values = recv[d, h, :, cols(k)]
            acc[h, 0] += lax.dot_general(values, wg[:, cols(k)], NT, preferred_element_type=F32)
            acc[h, 1] += lax.dot_general(values, wu[:, cols(k)], NT, preferred_element_type=F32)
            return carry

        lax.fori_loop(0, NK, step, 0)

    def forward_compute(h):
        gate_up(ONE, h)
        gate = acc[h, 0]
        hid[0] = (gate * jax.nn.sigmoid(gate) * acc[h, 1]).astype(BF16)

        def step(k, carry):
            part[0, h, :, cols(k)] = jnp.dot(hid[0], wd[:, cols(k)], preferred_element_type=F32).astype(BF16)
            return carry

        lax.fori_loop(0, NK, step, 0)
        fold(0, h)

    def backward_compute(h):
        unfold(GRADS, h)
        acc[h, 2] = jnp.zeros((ROWS, HID), F32)

        def down(k, carry):
            acc[h, 2] += lax.dot_general(recv[GRADS, h, :, cols(k)], wd[:, cols(k)], NT, preferred_element_type=F32)
            return carry

        lax.fori_loop(0, NK, down, 0)
        gate = acc[h, 0]
        sig = jax.nn.sigmoid(gate)
        slope = acc[h, 2] * sig
        hid[0] = (slope * acc[h, 1] * (1.0 + gate * (1.0 - sig))).astype(BF16)
        hid[1] = (slope * gate).astype(BF16)

        def step(k, carry):
            total = jnp.dot(hid[0], wg[:, cols(k)], preferred_element_type=F32)
            total = total + jnp.dot(hid[1], wu[:, cols(k)], preferred_element_type=F32)
            part[1, h, :, cols(k)] = total.astype(BF16)
            return carry

        lax.fori_loop(0, NK, step, 0)
        fold(1, h)

    def to_core(m, r):
        return pltpu.make_async_remote_copy(
            part.at[m, r // 2, pl.ds(pl.multiple_of(((r % 2) * 8 + (1 - c) * 4) * BLK, 64), 64)],
            cx.at[m, r],
            xsend.at[m, r],
            xrecv.at[m, r],
            device_id=(p, other),
            device_id_type=MESH,
        )

    def add_into(m, i, extra):
        r, source_z = source(i)
        h, b = place(r, c, source_z)
        part[m, h, rows16(b), :] = (part[m, h, rows16(b), :].astype(F32) + extra.astype(F32)).astype(BF16)

    def to_pair(m, i):
        r, source_z = source(i)
        h, b = place(r, c, source_z)
        return pltpu.make_async_remote_copy(
            part.at[m, h, rows16(b)],
            px.at[m, i],
            psend.at[m, i],
            precv.at[m, i],
            device_id=(p, pair),
            device_id_type=MESH,
        )

    def to_home(m, i):
        r, source_z = source(i)
        h, b = place(r, c, source_z)
        target = lax.rem(x + 4 - r, 4) * 8 + source_z * 2 + c
        src, dst, sem = part.at[m, h, rows16(b)], home.at[m, rows16(expert)], hrecv.at[m, expert]
        return target, src, dst, hsend.at[m, i], sem, (p, target)

    def leaves_here(i):
        return entry_own(source(i)[1], q) == z

    def return_first(m, half):
        for r in (half * 2, half * 2 + 1):
            pltpu.make_async_copy(cx.at[m, r], cx.at[m, r], xrecv.at[m, r]).wait()

            def step(i, carry):
                add_into(m, i, cx[m, r, rows16(source(i)[1]), :])

                @pl.when(jnp.logical_not(leaves_here(i)))
                def _():
                    to_pair(m, i).start()

                return carry

            lax.fori_loop(r * 4, r * 4 + 4, step, 0)

    def return_second(m, half):
        def step(i, carry):
            @pl.when(leaves_here(i))
            def _():
                pltpu.make_async_copy(px.at[m, i], px.at[m, i], precv.at[m, i]).wait()
                add_into(m, i, px[m, i])
                launch(to_home(m, i), True)

            return carry

        lax.fori_loop(half * 8, half * 8 + 8, step, 0)

    def collect(m, main_col, tail_col, prob_col, out):
        def step(e, carry):
            pltpu.make_async_copy(home.at[m, rows16(e)], home.at[m, rows16(e)], hrecv.at[m, e]).wait()
            return carry

        lax.fori_loop(0, EXPERTS, step, 0)
        row = iota((TOK, TOK), 1).astype(F32)
        table = onehot(row == main_col)
        tail = home[m, :, D:W]
        for k in range(NK):
            got = jnp.dot(table, home[m, :, k * KB : (k + 1) * KB], preferred_element_type=F32)
            got = got + jnp.dot(onehot(row == tail_col + 2.0 * k), tail, preferred_element_type=F32)
            if prob_col is not None:
                got = prob_col * got
            out[:, k * KB : (k + 1) * KB] = got.astype(BF16)

    loads[0].wait()
    fill(ACTS, main_row_two, tail_row_two, None)
    send(ACTS, 0, 8)
    loads[1].wait()
    metas[0].wait_recv()
    fill(ONE, meta_in[0, 0:1, :], meta_in[0, 1:2, :], None)
    send(ONE, 0, 8)
    forward(ACTS, 0, True)
    forward(ACTS, 1, True)
    forward(ONE, 0, True)
    forward(ONE, 1, True)
    loads[2].wait()
    metas[1].wait_recv()
    fill(GRADS, meta_in[1, 0:1, :], meta_in[1, 1:2, :], meta_in[1, 2:3, :])
    send(GRADS, 0, 8)
    for load in loads[3:]:
        load.wait()
    forward(ONE, 0, False)
    from_core(ONE, 0)
    forward_compute(0)
    to_core(0, 0).start()
    to_core(0, 1).start()
    forward(ONE, 1, False)
    return_first(0, 0)
    from_core(ONE, 1)
    forward_compute(1)
    to_core(0, 2).start()
    to_core(0, 3).start()
    forward(GRADS, 0, True)
    return_first(0, 1)
    forward(ACTS, 0, False)
    forward(ACTS, 1, False)
    from_core(ACTS, 0)
    gate_up(ACTS, 0)
    from_core(ACTS, 1)
    gate_up(ACTS, 1)
    forward(GRADS, 1, True)
    return_second(0, 0)
    forward(GRADS, 0, False)
    return_second(0, 1)
    from_core(GRADS, 0)
    backward_compute(0)
    to_core(1, 0).start()
    to_core(1, 1).start()
    forward(GRADS, 1, False)
    return_first(1, 0)
    from_core(GRADS, 1)
    backward_compute(1)
    to_core(1, 2).start()
    to_core(1, 3).start()
    return_first(1, 1)
    collect(0, main_col_one, tail_col_one, column(probs_one[...]), out_one)
    return_second(1, 0)
    return_second(1, 1)
    collect(1, main_col_two, tail_col_two, None, out_two)

    for copy in metas:
        copy.wait_send()

    for d in (ACTS, ONE, GRADS):

        def injected(i, carry):
            sent(dispatch(d, i), d == ACTS)
            return carry

        lax.fori_loop(0, EXPERTS, injected, 0)

        def passed(i, carry):
            @pl.when(entry(d, source(i)[1], q) == z)
            def _():
                onward(d, i, pair, fsend).wait_send()

            onward(d, i, other, csend).wait_send()
            return carry

        lax.fori_loop(0, 16, passed, 0)

    for m in range(2):
        for r in range(4):
            to_core(m, r).wait_send()

        def returned(i, carry):
            leaves = leaves_here(i)

            @pl.when(jnp.logical_not(leaves))
            def _():
                to_pair(m, i).wait_send()

            sent(to_home(m, i), True, leaves)
            return carry

        lax.fori_loop(0, 16, returned, 0)


def body(
    first_acts,
    first_routes,
    first_probs,
    second_acts,
    second_grads,
    second_routes,
    second_probs,
    gate_weight,
    up_weight,
    down_weight,
):
    vmem = pl.BlockSpec(memory_space=pltpu.VMEM)
    hbm = pl.BlockSpec(memory_space=pl.ANY)
    dma = pltpu.SemaphoreType.DMA
    result = jax.ShapeDtypeStruct((TOK, D), BF16)
    first_out, input_grads = pl.pallas_call(
        kernel,
        out_shape=(result, result),
        in_specs=[vmem] * 4 + [hbm] * 6,
        out_specs=(vmem, vmem),
        scratch_shapes=[
            pltpu.VMEM((3, TOK, D), BF16),
            pltpu.VMEM((HID, D), BF16),
            pltpu.VMEM((HID, D), BF16),
            pltpu.VMEM((HID, D), BF16),
            pltpu.VMEM((2, 8, TOK), F32),
            pltpu.VMEM((2, 8, TOK), F32),
            pltpu.VMEM((3, EXPERTS * BLK, W), BF16),
            pltpu.VMEM((3, 2, ROWS, W), BF16),
            pltpu.VMEM((2, 2, ROWS, W), BF16),
            pltpu.VMEM((2, 4, 4 * BLK, W), BF16),
            pltpu.VMEM((2, 16, BLK, W), BF16),
            pltpu.VMEM((2, EXPERTS * BLK, W), BF16),
            pltpu.VMEM((2, 3, ROWS, HID), F32),
            pltpu.VMEM((2, ROWS, HID), BF16),
            dma((6,)),
            dma((2,)),
            dma((2,)),
            dma((3, EXPERTS)),
            dma((3, 16)),
            dma((3, 16)),
            dma((3, SRC)),
            dma((2, 4)),
            dma((2, 4)),
            dma((2, 16)),
            dma((2, 16)),
            dma((2, 16)),
            dma((2, EXPERTS)),
        ],
        compiler_params=pltpu.CompilerParams(
            collective_id=0, has_side_effects=True, vmem_limit_bytes=63 * 1024 * 1024
        ),
    )(
        first_routes.reshape(1, TOK),
        first_probs.reshape(1, TOK),
        second_routes.reshape(1, TOK),
        second_probs.reshape(1, TOK),
        first_acts[0],
        second_acts[0],
        second_grads[0],
        gate_weight[0].T,
        up_weight[0].T,
        down_weight[0],
    )
    return (first_out[None], input_grads[None])


def solution(mesh):
    in_specs = (
        P("pipe", "ep", None),
        P("pipe", "ep", None),
        P("pipe", "ep", None),
        P("pipe", "ep", None),
        P("pipe", "ep", None),
        P("pipe", "ep", None),
        P("pipe", "ep", None),
        P("pipe", None, "ep"),
        P("pipe", None, "ep"),
        P("pipe", "ep", None),
    )
    out_specs = (P("pipe", "ep", None), P("pipe", "ep", None))
    return jax.shard_map(body, mesh=mesh, in_specs=in_specs, out_specs=out_specs, check_vma=False)
```

```python
import jax
import jax.numpy as jnp
from jax import lax
from jax.experimental import pallas as pl
from jax.experimental.pallas import tpu as pltpu
from jax.sharding import PartitionSpec as P

MESH = pl.DeviceIdType.MESH
F32 = jnp.float32
BF16 = jnp.bfloat16
NT = (((1,), (1,)), ((), ()))

TOK = 128
D = 4096
HID = 192
EXPERTS = 8
KB = 512
NK = D // KB
W = D + KB
BLK = 16
SRC = 32
SPLIT = 4
PIECE = HID // SPLIT
PIECES = 3 * SPLIT
HALF = SRC // 2
MAIN = HALF * BLK
EXTRA = HALF * 2
ROWS = MAIN + EXTRA
SECTIONS = 8

ONE, ACTS, GRADS = 0, 1, 2


def rows16(index):
    return pl.ds(pl.multiple_of(index * BLK, BLK), BLK)


def cols(index):
    return pl.ds(pl.multiple_of(index * KB, KB), KB)


def iota(shape, dim):
    return lax.broadcasted_iota(jnp.int32, shape, dim)


def onehot(mask):
    return jnp.where(mask, 1.0, 0.0).astype(BF16)


def column(row):
    eye = iota((TOK, TOK), 0) == iota((TOK, TOK), 1)
    return jnp.sum(jnp.where(eye, jnp.broadcast_to(row, (TOK, TOK)), 0.0), axis=1, keepdims=True)


def codes(expert_row):
    here, there = iota((TOK, TOK), 0), iota((TOK, TOK), 1)
    row = expert_row.astype(F32)
    col = column(row)
    same = jnp.where(col == row, 1.0, 0.0)
    slot_col = jnp.sum(jnp.where(there < here, same, 0.0), axis=1, keepdims=True)
    slot_row = jnp.sum(jnp.where(here < there, same, 0.0), axis=0, keepdims=True)

    def both(expert, slot):
        main = jnp.where(slot < BLK, expert * BLK + slot, -1.0)
        tail = jnp.where(slot < BLK, -1024.0, expert * BLK + slot - BLK)
        return main, tail

    return both(col, slot_col), both(row, slot_row)


def flip(z, k):
    return (z % 2 + k % 2) % 2 + 2 * ((z // 2 + k // 2) % 2)


def kernel(
    routes_one, probs_one, routes_two, probs_two, one_hbm, acts_hbm, grads_hbm, gate_hbm, up_hbm, down_hbm,
    out_one, out_two,
    held, held_w, meta_out, meta_in, stage, recv, part, cx, px, home, acc, hid, relay,
    load_sem, msend, mrecv, dsend, fsend, csend, rsem, xsend, xrecv, psend, precv, hsend, hrecv,
    wsend, wrecv, relay_recv, out_sem,
):
    p, j = lax.axis_index("pipe"), lax.axis_index("ep")
    x, z, c = j // 8, (j // 2) % 4, j % 2
    columns = x // 2
    flipped_x, flipped_z = flip(x, 1), flip(z, 1)
    expert = (columns * 2 + z % 2) * 2 + z // 2
    other = x * 8 + z * 2 + (1 - c)
    pair = flipped_x * 8 + z * 2 + c
    even = x % 2 == z % 2
    relays = jnp.logical_and(c == 1, even)
    round_x, round_z = jnp.where(even, flipped_x, x), jnp.where(even, z, flipped_z)
    beside = flipped_x * 8 + z * 2 + 1
    beyond = x * 8 + flipped_z * 2 + 1
    after, before = lax.rem(p + 1, SECTIONS), lax.rem(p + SECTIONS - 1, SECTIONS)
    section = {ONE: after, ACTS: p, GRADS: before}

    loads = [
        pltpu.make_async_copy(src, held.at[d], load_sem.at[d])
        for d, src in ((ACTS, acts_hbm), (ONE, one_hbm), (GRADS, grads_hbm))
    ]
    for load in loads:
        load.start()

    weights = (gate_hbm, up_hbm, down_hbm)

    def slot(i, n):
        return held_w.at[i, pl.ds(n * PIECE, PIECE)]

    def keep_weights():
        for i in range(3):
            for n in range(SPLIT):
                src = weights[i].at[pl.ds(n * PIECE, PIECE)]
                pl.when(relays)(pltpu.make_async_copy(src, slot(i, n), wrecv.at[i * SPLIT + n]).start)

    def give_weight(i, n):
        part_of, t = pl.ds(pl.multiple_of(n * PIECE, BLK), PIECE), i * SPLIT + n
        src = weights[i].at[part_of]

        @pl.when(c == 0)
        def _():
            pltpu.make_async_remote_copy(
                src, held_w.at[i, part_of], wsend.at[t], wrecv.at[t],
                device_id=(p, round_x * 8 + round_z * 2), device_id_type=MESH,
            ).start()

        @pl.when(jnp.logical_and(c == 1, jnp.logical_not(even)))
        def _():
            pltpu.make_async_remote_copy(
                src, relay.at[t], wsend.at[t], relay_recv.at[t], device_id=(p, beside), device_id_type=MESH
            ).start()

    def give_all(i):
        def step(n, carry):
            give_weight(i, n)
            return carry

        lax.fori_loop(0, SPLIT, step, 0)

    def relay_weight(t):
        @pl.when(relays)
        def _():
            pltpu.make_async_copy(relay.at[t], relay.at[t], relay_recv.at[t]).wait()
            pltpu.make_async_remote_copy(
                relay.at[t],
                held_w.at[t // SPLIT, pl.ds(pl.multiple_of((t % SPLIT) * PIECE, BLK), PIECE)],
                wsend.at[t],
                wrecv.at[t],
                device_id=(p, beyond),
                device_id_type=MESH,
            ).start()

    def weights_here():
        for i in range(3):
            for n in range(SPLIT):
                pltpu.make_async_copy(slot(i, n), slot(i, n), wrecv.at[i * SPLIT + n]).wait()

    barrier = pltpu.get_barrier_semaphore()

    def greet(n, carry):
        them = (n // 4) * 8 + (n % 4) * 2 + c
        pl.semaphore_signal(barrier, inc=1, device_id=(after, them), device_id_type=MESH)
        pl.semaphore_signal(barrier, inc=1, device_id=(before, them), device_id_type=MESH)

        @pl.when(them != j)
        def _():
            pl.semaphore_signal(barrier, inc=1, device_id=(p, them), device_id_type=MESH)

        return carry

    lax.fori_loop(0, 16, greet, 0)
    pl.semaphore_signal(barrier, inc=1, device_id=(p, other), device_id_type=MESH)

    (main_col_one, tail_col_one), (main_row_one, tail_row_one) = codes(routes_one[...])
    (main_col_two, tail_col_two), (main_row_two, tail_row_two) = codes(routes_two[...])
    meta_out[0, 0:1, :] = main_row_one
    meta_out[0, 1:2, :] = tail_row_one
    meta_out[0, 2:8, :] = jnp.zeros((6, TOK), F32)
    meta_out[1, 0:1, :] = main_row_two
    meta_out[1, 1:2, :] = tail_row_two
    meta_out[1, 2:3, :] = probs_two[...]
    meta_out[1, 3:8, :] = jnp.zeros((5, TOK), F32)

    pl.semaphore_wait(barrier, 48)

    metas = [
        pltpu.make_async_remote_copy(
            meta_out.at[i], meta_in.at[i], msend.at[i], mrecv.at[i], device_id=(to, j), device_id_type=MESH
        )
        for i, to in enumerate((before, after))
    ]
    for copy in metas:
        copy.start()

    def fill(d, main_row, tail_row, prob_row):
        row = iota((TOK, TOK), 0).astype(F32)
        here = row == main_row
        table = onehot(here)
        tail = jnp.zeros((TOK, KB), F32)
        tail_prob = jnp.zeros((TOK, 1), F32)
        if prob_row is not None:
            prob = jnp.sum(jnp.where(here, prob_row, 0.0), axis=1, keepdims=True)
        for k in range(NK):
            values = held[d, :, k * KB : (k + 1) * KB]
            got = jnp.dot(table, values, preferred_element_type=F32)
            there = row == tail_row + 2.0 * k
            tail = tail + jnp.dot(onehot(there), values, preferred_element_type=F32)
            if prob_row is not None:
                got = prob * got
                tail_prob = tail_prob + jnp.sum(jnp.where(there, prob_row, 0.0), axis=1, keepdims=True)
            stage[d, :, k * KB : (k + 1) * KB] = got.astype(BF16)
        if prob_row is not None:
            tail = tail_prob * tail
        stage[d, :, D:W] = tail.astype(BF16)

    def place(parity, core, source_z):
        return parity * 8 + core * 4 + source_z

    def enters(half):
        return (x + half) % 2

    def launch(move, may_stay):
        target, src, dst, send_sem, sem, device = move

        def remote():
            pltpu.make_async_remote_copy(src, dst, send_sem, sem, device_id=device, device_id_type=MESH).start()

        if not may_stay:
            remote()
            return
        pl.when(target != j)(remote)

        @pl.when(target == j)
        def _():
            pltpu.make_async_copy(src, dst, sem).start()

    def sent(move, may_stay):
        target, src, dst, send_sem, sem, device = move

        def wait():
            pltpu.make_async_remote_copy(src, dst, send_sem, sem, device_id=device, device_id_type=MESH).wait_send()

        if may_stay:
            pl.when(target != j)(wait)
        else:
            wait()

    def dispatch(d, i):
        half = i // 4
        to_z = flip(z, i % 4 if d == ACTS else 3 - i % 4)
        to_columns = jnp.where(half == 0, columns, 1 - columns)
        target = jnp.where(half == 0, x, 3 - x) * 8 + to_z * 2 + c
        e = (to_columns * 2 + to_z % 2) * 2 + to_z // 2
        b = place(x % 2, c, z)
        sem = rsem.at[d, half * HALF + b]
        src, dst = stage.at[d, rows16(e)], recv.at[d, half, rows16(b)]
        return target, src, dst, dsend.at[d, i], sem, (section[d], target)

    def send(d, low, high):
        def step(i, carry):
            launch(dispatch(d, i), d == ACTS)
            return carry

        lax.fori_loop(low, high, step, 0)

    def arrived(d, h, b):
        ref = recv.at[d, h, rows16(b)]
        pltpu.make_async_copy(ref, ref, rsem.at[d, h * HALF + b]).wait()

    def onward(d, half, b, to, sem):
        ref = recv.at[d, half, rows16(b)]
        return pltpu.make_async_remote_copy(
            ref, ref, sem, rsem.at[d, half * HALF + b], device_id=(p, to), device_id_type=MESH
        )

    def to_pair_sem(d, half, source_z):
        return fsend.at[d, half * 4 + source_z]

    def to_core_sem(d, half, parity, source_z):
        return csend.at[d, half * 8 + parity * 4 + source_z]

    def forward(d, half, direct, give=None, relay_of=None):
        parity = enters(half) if direct else 1 - enters(half)

        def step(k, carry):
            source_z = flip(z, k if d == ACTS else 3 - k)
            b = place(parity, c, source_z)
            arrived(d, half, b)
            if direct:
                onward(d, half, b, pair, to_pair_sem(d, half, source_z)).start()
            onward(d, half, b, other, to_core_sem(d, half, parity, source_z)).start()
            if give is not None:
                give_weight(give, k)
            if relay_of is not None:
                relay_weight(relay_of * SPLIT + k)
            return carry

        lax.fori_loop(0, 4, step, 0)

    def from_core(d, half):
        def step(k, carry):
            arrived(d, half, place(k // 4, 1 - c, k % 4))
            return carry

        lax.fori_loop(0, 8, step, 0)

    def unfold(d, h):
        row, col = iota((EXTRA, MAIN), 0), iota((EXTRA, MAIN), 1)
        base = (row // 2) * BLK + row % 2
        tail = recv[d, h, 0:MAIN, D:W]
        for k in range(NK):
            pick = onehot(col == base + 2 * k)
            recv[d, h, MAIN:ROWS, k * KB : (k + 1) * KB] = jnp.dot(pick, tail, preferred_element_type=F32).astype(BF16)

    def fold(m, h):
        row, col = iota((MAIN, EXTRA), 0), iota((MAIN, EXTRA), 1)
        base = (col // 2) * BLK + col % 2
        tail = jnp.zeros((MAIN, KB), F32)
        for k in range(NK):
            pick = onehot(row == base + 2 * k)
            tail = tail + jnp.dot(pick, part[m, h, MAIN:ROWS, k * KB : (k + 1) * KB], preferred_element_type=F32)
        part[m, h, 0:MAIN, D:W] = tail.astype(BF16)

    def gate_up(d, h):
        unfold(d, h)
        acc[h, 0:2] = jnp.zeros((2, ROWS, HID), F32)

        def step(k, carry):
            values = recv[d, h, :, cols(k)]
            acc[h, 0] += lax.dot_general(values, held_w[0, :, cols(k)], NT, preferred_element_type=F32)
            acc[h, 1] += lax.dot_general(values, held_w[1, :, cols(k)], NT, preferred_element_type=F32)
            return carry

        lax.fori_loop(0, NK, step, 0)

    def forward_compute(h):
        gate_up(ONE, h)
        gate = acc[h, 0]
        hid[0] = (gate * jax.nn.sigmoid(gate) * acc[h, 1]).astype(BF16)

        def step(k, carry):
            part[0, h, :, cols(k)] = jnp.dot(hid[0], held_w[2, :, cols(k)], preferred_element_type=F32).astype(BF16)
            return carry

        lax.fori_loop(0, NK, step, 0)
        fold(0, h)

    def backward_hidden(h):
        unfold(GRADS, h)
        acc[h, 2] = jnp.zeros((ROWS, HID), F32)

        def down(k, carry):
            acc[h, 2] += lax.dot_general(recv[GRADS, h, :, cols(k)], held_w[2, :, cols(k)], NT, preferred_element_type=F32)
            return carry

        lax.fori_loop(0, NK, down, 0)
        gate = acc[h, 0]
        sig = jax.nn.sigmoid(gate)
        slope = acc[h, 2] * sig
        hid[0] = (slope * acc[h, 1] * (1.0 + gate * (1.0 - sig))).astype(BF16)
        hid[1] = (slope * gate).astype(BF16)

    def backward_rows(h):
        def step(k, carry):
            total = jnp.dot(hid[0], held_w[0, :, cols(k)], preferred_element_type=F32)
            total = total + jnp.dot(hid[1], held_w[1, :, cols(k)], preferred_element_type=F32)
            part[1, h, :, cols(k)] = total.astype(BF16)
            return carry

        lax.fori_loop(0, NK, step, 0)
        fold(1, h)

    def to_core(m, half, parity):
        n = half * 2 + parity
        return pltpu.make_async_remote_copy(
            part.at[m, half, pl.ds(pl.multiple_of(place(parity, 1 - c, 0) * BLK, 64), 64)],
            cx.at[m, n],
            xsend.at[m, n],
            xrecv.at[m, n],
            device_id=(p, other),
            device_id_type=MESH,
        )

    def exchange(m, half):
        to_core(m, half, 1 - enters(half)).start()
        to_core(m, half, enters(half)).start()

    def add_into(m, half, b, extra):
        mine = part[m, half, rows16(b), :]
        part[m, half, rows16(b), :] = (mine.astype(F32) + extra.astype(F32)).astype(BF16)

    def to_pair(m, half, source_z):
        n = half * 4 + source_z
        return pltpu.make_async_remote_copy(
            part.at[m, half, rows16(place(1 - enters(half), c, source_z))],
            px.at[m, n],
            psend.at[m, n],
            precv.at[m, n],
            device_id=(p, pair),
            device_id_type=MESH,
        )

    def to_home(m, half, source_z):
        b = place(enters(half), c, source_z)
        target = (x if half == 0 else 3 - x) * 8 + source_z * 2 + c
        src, dst, sem = part.at[m, half, rows16(b)], home.at[m, rows16(expert)], hrecv.at[m, expert]
        return target, src, dst, hsend.at[m, half * 4 + source_z], sem, (p, target)

    def return_first(m, half):
        for parity, leaves in ((1 - enters(half), False), (enters(half), True)):
            n = half * 2 + parity
            pltpu.make_async_copy(cx.at[m, n], cx.at[m, n], xrecv.at[m, n]).wait()

            def step(k, carry):
                source_z = flip(z, 3 - k)
                add_into(m, half, place(parity, c, source_z), cx[m, n, rows16(source_z), :])
                if not leaves:
                    to_pair(m, half, source_z).start()
                return carry

            lax.fori_loop(0, 4, step, 0)

    def return_second(m, half):
        def step(k, carry):
            source_z = flip(z, 3 - k)
            n = half * 4 + source_z
            pltpu.make_async_copy(px.at[m, n], px.at[m, n], precv.at[m, n]).wait()
            add_into(m, half, place(enters(half), c, source_z), px[m, n])
            launch(to_home(m, half, source_z), half == 0)
            return carry

        lax.fori_loop(0, 4, step, 0)

    def drain_dispatch(d):
        def injected(i, carry):
            sent(dispatch(d, i), d == ACTS)
            return carry

        lax.fori_loop(0, EXPERTS, injected, 0)
        for half in range(2):

            def passed(k, carry):
                onward(d, half, place(enters(half), c, k), pair, to_pair_sem(d, half, k)).wait_send()
                for parity in range(2):
                    onward(d, half, place(parity, c, k), other, to_core_sem(d, half, parity, k)).wait_send()
                return carry

            lax.fori_loop(0, 4, passed, 0)

    def drain_return(m):
        for half in range(2):
            to_core(m, half, 0).wait_send()
            to_core(m, half, 1).wait_send()

            def returned(k, carry):
                to_pair(m, half, k).wait_send()
                sent(to_home(m, half, k), half == 0)
                return carry

            lax.fori_loop(0, 4, returned, 0)

    def drain_weights():
        def gone(t, carry):
            pltpu.make_async_remote_copy(
                relay.at[t], relay.at[t], wsend.at[t], wrecv.at[t], device_id=(p, beside), device_id_type=MESH
            ).wait_send()
            return carry

        lax.fori_loop(0, PIECES, gone, 0)

    def result(m, n, out):
        part_of = pl.ds(n * (D // 2), D // 2)
        return pltpu.make_async_copy(held.at[m, :, part_of], out.at[:, part_of], out_sem.at[m, n])

    def collect(m, main_col, tail_col, prob_col, out):
        def step(e, carry):
            pltpu.make_async_copy(home.at[m, rows16(e)], home.at[m, rows16(e)], hrecv.at[m, e]).wait()
            return carry

        lax.fori_loop(0, EXPERTS, step, 0)
        row = iota((TOK, TOK), 1).astype(F32)
        table = onehot(row == main_col)
        tail = home[m, :, D:W]
        for k in range(NK):
            got = jnp.dot(table, home[m, :, k * KB : (k + 1) * KB], preferred_element_type=F32)
            got = got + jnp.dot(onehot(row == tail_col + 2.0 * k), tail, preferred_element_type=F32)
            if prob_col is not None:
                got = prob_col * got
            held[m, :, k * KB : (k + 1) * KB] = got.astype(BF16)
            if k % 4 == 3:
                result(m, k // 4, out).start()

    loads[0].wait()
    fill(ACTS, main_row_two, tail_row_two, None)
    send(ACTS, 0, 8)
    keep_weights()
    loads[1].wait()
    metas[0].wait_recv()
    fill(ONE, meta_in[0, 0:1, :], meta_in[0, 1:2, :], None)
    send(ONE, 0, 8)
    give_all(0)
    give_all(1)
    give_all(2)
    forward(ACTS, 0, True, None, None)
    forward(ACTS, 1, True, None, 0)
    forward(ONE, 0, True, None, 1)
    forward(ONE, 1, True, None, 2)
    loads[2].wait()
    metas[1].wait_recv()
    fill(GRADS, meta_in[1, 0:1, :], meta_in[1, 1:2, :], meta_in[1, 2:3, :])
    send(GRADS, 0, 8)
    forward(ONE, 0, False)
    from_core(ONE, 0)
    forward(ONE, 1, False)
    forward(ACTS, 0, False)
    forward(ACTS, 1, False)
    forward(GRADS, 0, True)
    weights_here()
    forward_compute(0)
    exchange(0, 0)
    forward(GRADS, 1, True)
    from_core(ONE, 1)
    forward_compute(1)
    exchange(0, 1)
    return_first(0, 0)
    return_first(0, 1)
    from_core(ACTS, 0)
    forward(GRADS, 0, False)
    gate_up(ACTS, 0)
    from_core(ACTS, 1)
    forward(GRADS, 1, False)
    gate_up(ACTS, 1)
    from_core(GRADS, 0)
    backward_hidden(0)
    backward_rows(0)
    exchange(1, 0)
    return_second(0, 0)
    from_core(GRADS, 1)
    backward_hidden(1)
    return_first(1, 0)
    backward_rows(1)
    exchange(1, 1)
    return_second(0, 1)
    return_first(1, 1)
    return_second(1, 0)
    drain_dispatch(ACTS)
    drain_dispatch(ONE)
    drain_dispatch(GRADS)
    drain_weights()
    for copy in metas:
        copy.wait_send()
    return_second(1, 1)
    drain_return(0)
    collect(0, main_col_one, tail_col_one, column(probs_one[...]), out_one)
    collect(1, main_col_two, tail_col_two, None, out_two)
    drain_return(1)
    for n in range(2):
        result(0, n, out_one).wait()
        result(1, n, out_two).wait()


def body(
    first_acts,
    first_routes,
    first_probs,
    second_acts,
    second_grads,
    second_routes,
    second_probs,
    gate_weight,
    up_weight,
    down_weight,
):
    vmem = pl.BlockSpec(memory_space=pltpu.VMEM)
    hbm = pl.BlockSpec(memory_space=pl.ANY)
    dma = pltpu.SemaphoreType.DMA
    result = jax.ShapeDtypeStruct((TOK, D), BF16)
    first_out, input_grads = pl.pallas_call(
        kernel,
        out_shape=(result, result),
        in_specs=[vmem] * 4 + [hbm] * 6,
        out_specs=(hbm, hbm),
        scratch_shapes=[
            pltpu.VMEM((3, TOK, D), BF16),
            pltpu.VMEM((3, HID, D), BF16),
            pltpu.VMEM((2, 8, TOK), F32),
            pltpu.VMEM((2, 8, TOK), F32),
            pltpu.VMEM((3, EXPERTS * BLK, W), BF16),
            pltpu.VMEM((3, 2, ROWS, W), BF16),
            pltpu.VMEM((2, 2, ROWS, W), BF16),
            pltpu.VMEM((2, 4, 4 * BLK, W), BF16),
            pltpu.VMEM((2, 8, BLK, W), BF16),
            pltpu.VMEM((2, EXPERTS * BLK, W), BF16),
            pltpu.VMEM((2, 3, ROWS, HID), F32),
            pltpu.VMEM((2, ROWS, HID), BF16),
            pltpu.VMEM((PIECES, PIECE, D), BF16),
            dma((3,)),
            dma((2,)),
            dma((2,)),
            dma((3, EXPERTS)),
            dma((3, 8)),
            dma((3, 16)),
            dma((3, SRC)),
            dma((2, 4)),
            dma((2, 4)),
            dma((2, 8)),
            dma((2, 8)),
            dma((2, 8)),
            dma((2, EXPERTS)),
            dma((PIECES,)),
            dma((PIECES,)),
            dma((PIECES,)),
            dma((2, 2)),
        ],
        compiler_params=pltpu.CompilerParams(
            collective_id=0, has_side_effects=True, vmem_limit_bytes=63 * 1024 * 1024
        ),
    )(
        first_routes.reshape(1, TOK),
        first_probs.reshape(1, TOK),
        second_routes.reshape(1, TOK),
        second_probs.reshape(1, TOK),
        first_acts[0],
        second_acts[0],
        second_grads[0],
        gate_weight[0].T,
        up_weight[0].T,
        down_weight[0],
    )
    return (first_out[None], input_grads[None])


def solution(mesh):
    in_specs = (
        P("pipe", "ep", None),
        P("pipe", "ep", None),
        P("pipe", "ep", None),
        P("pipe", "ep", None),
        P("pipe", "ep", None),
        P("pipe", "ep", None),
        P("pipe", "ep", None),
        P("pipe", None, "ep"),
        P("pipe", None, "ep"),
        P("pipe", "ep", None),
    )
    out_specs = (P("pipe", "ep", None), P("pipe", "ep", None))
    return jax.shard_map(body, mesh=mesh, in_specs=in_specs, out_specs=out_specs, check_vma=False)
```

```python
import jax
import jax.numpy as jnp
from jax import lax
from jax.experimental import pallas as pl
from jax.experimental.pallas import tpu as pltpu
from jax.sharding import PartitionSpec as P

MESH = pl.DeviceIdType.MESH
F32 = jnp.float32
BF16 = jnp.bfloat16
NT = (((1,), (1,)), ((), ()))

TOK = 128
D = 4096
HID = 192
EXPERTS = 8
KB = 512
NK = D // KB
WIDE = 1024
W = D + KB
BLK = 16
SRC = 32
SPLIT = 4
PIECE = HID // SPLIT
PIECES = 3 * SPLIT
HALF = SRC // 2
MAIN = HALF * BLK
EXTRA = HALF * 2
ROWS = MAIN + EXTRA
SECTIONS = 8

ONE, ACTS, GRADS = 0, 1, 2


def rows16(index):
    return pl.ds(pl.multiple_of(index * BLK, BLK), BLK)


def cols(index):
    return pl.ds(pl.multiple_of(index * KB, KB), KB)


def wide(index):
    return pl.ds(pl.multiple_of(index * WIDE, WIDE), WIDE)


def iota(shape, dim):
    return lax.broadcasted_iota(jnp.int32, shape, dim)


def onehot(mask):
    return jnp.where(mask, 1.0, 0.0).astype(BF16)


def column(row):
    eye = iota((TOK, TOK), 0) == iota((TOK, TOK), 1)
    return jnp.sum(jnp.where(eye, jnp.broadcast_to(row, (TOK, TOK)), 0.0), axis=1, keepdims=True)


def codes(expert_row):
    here, there = iota((TOK, TOK), 0), iota((TOK, TOK), 1)
    row = expert_row.astype(F32)
    col = column(row)
    same = jnp.where(col == row, 1.0, 0.0)
    slot_col = jnp.sum(jnp.where(there < here, same, 0.0), axis=1, keepdims=True)
    slot_row = jnp.sum(jnp.where(here < there, same, 0.0), axis=0, keepdims=True)

    def both(expert, slot):
        main = jnp.where(slot < BLK, expert * BLK + slot, -1.0)
        tail = jnp.where(slot < BLK, -1024.0, expert * BLK + slot - BLK)
        return main, tail

    return both(col, slot_col), both(row, slot_row)


def flip(z, k):
    return (z % 2 + k % 2) % 2 + 2 * ((z // 2 + k // 2) % 2)


def kernel(
    routes_one, probs_one, routes_two, probs_two, one_hbm, acts_hbm, grads_hbm, gate_hbm, up_hbm, down_hbm,
    out_one, out_two,
    held, held_w, meta_out, meta_in, stage, recv, part, cx, px, home, acc, hid, relay,
    load_sem, msend, mrecv, dsend, fsend, csend, rsem, xsend, xrecv, psend, precv, hsend, hrecv,
    wsend, wrecv, relay_recv, out_sem,
):
    p, j = lax.axis_index("pipe"), lax.axis_index("ep")
    x, z, c = j // 8, (j // 2) % 4, j % 2
    columns = x // 2
    flipped_x, flipped_z = flip(x, 1), flip(z, 1)
    expert = (columns * 2 + z % 2) * 2 + z // 2
    other = x * 8 + z * 2 + (1 - c)
    pair = flipped_x * 8 + z * 2 + c
    even = x % 2 == z % 2
    relays = jnp.logical_and(c == 1, even)
    round_x, round_z = jnp.where(even, flipped_x, x), jnp.where(even, z, flipped_z)
    beside = flipped_x * 8 + z * 2 + 1
    beyond = x * 8 + flipped_z * 2 + 1
    after, before = lax.rem(p + 1, SECTIONS), lax.rem(p + SECTIONS - 1, SECTIONS)
    section = {ONE: after, ACTS: p, GRADS: before}

    loads = [
        pltpu.make_async_copy(src, held.at[d], load_sem.at[d])
        for d, src in ((ACTS, acts_hbm), (ONE, one_hbm), (GRADS, grads_hbm))
    ]
    for load in loads:
        load.start()

    weights = (gate_hbm, up_hbm, down_hbm)

    def slot(i, n):
        return held_w.at[i, pl.ds(n * PIECE, PIECE)]

    def keep_weights():
        for i in range(3):
            for n in range(SPLIT):
                src = weights[i].at[pl.ds(n * PIECE, PIECE)]
                pl.when(relays)(pltpu.make_async_copy(src, slot(i, n), wrecv.at[i * SPLIT + n]).start)

    def give_weight(i, n):
        part_of, t = pl.ds(pl.multiple_of(n * PIECE, BLK), PIECE), i * SPLIT + n
        src = weights[i].at[part_of]

        @pl.when(c == 0)
        def _():
            pltpu.make_async_remote_copy(
                src, held_w.at[i, part_of], wsend.at[t], wrecv.at[t],
                device_id=(p, round_x * 8 + round_z * 2), device_id_type=MESH,
            ).start()

        @pl.when(jnp.logical_and(c == 1, jnp.logical_not(even)))
        def _():
            pltpu.make_async_remote_copy(
                src, relay.at[t], wsend.at[t], relay_recv.at[t], device_id=(p, beside), device_id_type=MESH
            ).start()

    def give_all(i):
        def step(n, carry):
            give_weight(i, n)
            return carry

        lax.fori_loop(0, SPLIT, step, 0)

    def relay_weight(t):
        @pl.when(relays)
        def _():
            pltpu.make_async_copy(relay.at[t], relay.at[t], relay_recv.at[t]).wait()
            pltpu.make_async_remote_copy(
                relay.at[t],
                held_w.at[t // SPLIT, pl.ds(pl.multiple_of((t % SPLIT) * PIECE, BLK), PIECE)],
                wsend.at[t],
                wrecv.at[t],
                device_id=(p, beyond),
                device_id_type=MESH,
            ).start()

    def weights_here():
        for i in range(3):
            for n in range(SPLIT):
                pltpu.make_async_copy(slot(i, n), slot(i, n), wrecv.at[i * SPLIT + n]).wait()

    barrier = pltpu.get_barrier_semaphore()

    def greet(n, carry):
        them = (n // 4) * 8 + (n % 4) * 2 + c
        pl.semaphore_signal(barrier, inc=1, device_id=(after, them), device_id_type=MESH)
        pl.semaphore_signal(barrier, inc=1, device_id=(before, them), device_id_type=MESH)

        @pl.when(them != j)
        def _():
            pl.semaphore_signal(barrier, inc=1, device_id=(p, them), device_id_type=MESH)

        return carry

    lax.fori_loop(0, 16, greet, 0)
    pl.semaphore_signal(barrier, inc=1, device_id=(p, other), device_id_type=MESH)

    (main_col_one, tail_col_one), (main_row_one, tail_row_one) = codes(routes_one[...])
    (main_col_two, tail_col_two), (main_row_two, tail_row_two) = codes(routes_two[...])
    meta_out[0, 0:1, :] = main_row_one
    meta_out[0, 1:2, :] = tail_row_one
    meta_out[0, 2:8, :] = jnp.zeros((6, TOK), F32)
    meta_out[1, 0:1, :] = main_row_two
    meta_out[1, 1:2, :] = tail_row_two
    meta_out[1, 2:3, :] = probs_two[...]
    meta_out[1, 3:8, :] = jnp.zeros((5, TOK), F32)

    pl.semaphore_wait(barrier, 48)

    metas = [
        pltpu.make_async_remote_copy(
            meta_out.at[i], meta_in.at[i], msend.at[i], mrecv.at[i], device_id=(to, j), device_id_type=MESH
        )
        for i, to in enumerate((before, after))
    ]
    for copy in metas:
        copy.start()

    def fill(d, main_row, tail_row, prob_row):
        row = iota((TOK, TOK), 0).astype(F32)
        here = row == main_row
        table = onehot(here)
        tail = jnp.zeros((TOK, KB), F32)
        tail_prob = jnp.zeros((TOK, 1), F32)
        if prob_row is not None:
            prob = jnp.sum(jnp.where(here, prob_row, 0.0), axis=1, keepdims=True)
        for k in range(NK):
            values = held[d, :, k * KB : (k + 1) * KB]
            got = jnp.dot(table, values, preferred_element_type=F32)
            there = row == tail_row + 2.0 * k
            tail = tail + jnp.dot(onehot(there), values, preferred_element_type=F32)
            if prob_row is not None:
                got = prob * got
                tail_prob = tail_prob + jnp.sum(jnp.where(there, prob_row, 0.0), axis=1, keepdims=True)
            stage[d, :, k * KB : (k + 1) * KB] = got.astype(BF16)
        if prob_row is not None:
            tail = tail_prob * tail
        stage[d, :, D:W] = tail.astype(BF16)

    def place(parity, core, source_z):
        return parity * 8 + core * 4 + source_z

    def enters(half):
        return (x + half) % 2

    def launch(move, may_stay):
        target, src, dst, send_sem, sem, device = move

        def remote():
            pltpu.make_async_remote_copy(src, dst, send_sem, sem, device_id=device, device_id_type=MESH).start()

        if not may_stay:
            remote()
            return
        pl.when(target != j)(remote)

        @pl.when(target == j)
        def _():
            pltpu.make_async_copy(src, dst, sem).start()

    def sent(move, may_stay):
        target, src, dst, send_sem, sem, device = move

        def wait():
            pltpu.make_async_remote_copy(src, dst, send_sem, sem, device_id=device, device_id_type=MESH).wait_send()

        if may_stay:
            pl.when(target != j)(wait)
        else:
            wait()

    def dispatch(d, i):
        half = i // 4
        to_z = flip(z, i % 4 if d == ACTS else 3 - i % 4)
        to_columns = jnp.where(half == 0, columns, 1 - columns)
        target = jnp.where(half == 0, x, 3 - x) * 8 + to_z * 2 + c
        e = (to_columns * 2 + to_z % 2) * 2 + to_z // 2
        b = place(x % 2, c, z)
        sem = rsem.at[d, half * HALF + b]
        src, dst = stage.at[d, rows16(e)], recv.at[d, half, rows16(b)]
        return target, src, dst, dsend.at[d, i], sem, (section[d], target)

    def send(d, low, high):
        def step(i, carry):
            launch(dispatch(d, i), d == ACTS)
            return carry

        lax.fori_loop(low, high, step, 0)

    def arrived(d, h, b):
        ref = recv.at[d, h, rows16(b)]
        pltpu.make_async_copy(ref, ref, rsem.at[d, h * HALF + b]).wait()

    def onward(d, half, b, to, sem):
        ref = recv.at[d, half, rows16(b)]
        return pltpu.make_async_remote_copy(
            ref, ref, sem, rsem.at[d, half * HALF + b], device_id=(p, to), device_id_type=MESH
        )

    def to_pair_sem(d, half, source_z):
        return fsend.at[d, half * 4 + source_z]

    def to_core_sem(d, half, parity, source_z):
        return csend.at[d, half * 8 + parity * 4 + source_z]

    def forward(d, half, direct, give=None, relay_of=None):
        parity = enters(half) if direct else 1 - enters(half)

        def step(k, carry):
            source_z = flip(z, k if d == ACTS else 3 - k)
            b = place(parity, c, source_z)
            arrived(d, half, b)
            if direct:
                onward(d, half, b, pair, to_pair_sem(d, half, source_z)).start()
            onward(d, half, b, other, to_core_sem(d, half, parity, source_z)).start()
            if give is not None:
                give_weight(give, k)
            if relay_of is not None:
                relay_weight(relay_of * SPLIT + k)
            return carry

        lax.fori_loop(0, 4, step, 0)

    def from_core(d, half):
        def step(k, carry):
            arrived(d, half, place(k // 4, 1 - c, k % 4))
            return carry

        lax.fori_loop(0, 8, step, 0)

    def unfold(d, h):
        row, col = iota((EXTRA, MAIN), 0), iota((EXTRA, MAIN), 1)
        base = (row // 2) * BLK + row % 2
        tail = recv[d, h, 0:MAIN, D:W]
        for k in range(NK):
            pick = onehot(col == base + 2 * k)
            recv[d, h, MAIN:ROWS, k * KB : (k + 1) * KB] = jnp.dot(pick, tail, preferred_element_type=F32).astype(BF16)

    def fold(m, h):
        row, col = iota((MAIN, EXTRA), 0), iota((MAIN, EXTRA), 1)
        base = (col // 2) * BLK + col % 2
        tail = jnp.zeros((MAIN, KB), F32)
        for k in range(NK):
            pick = onehot(row == base + 2 * k)
            tail = tail + jnp.dot(pick, part[m, h, MAIN:ROWS, k * KB : (k + 1) * KB], preferred_element_type=F32)
        part[m, h, 0:MAIN, D:W] = tail.astype(BF16)

    def gate_up(d, h):
        unfold(d, h)
        acc[h, 0:2] = jnp.zeros((2, ROWS, HID), F32)

        def step(k, carry):
            values = recv[d, h, :, wide(k)]
            acc[h, 0] += lax.dot_general(values, held_w[0, :, wide(k)], NT, preferred_element_type=F32)
            acc[h, 1] += lax.dot_general(values, held_w[1, :, wide(k)], NT, preferred_element_type=F32)
            return carry

        lax.fori_loop(0, D // WIDE, step, 0)

    def forward_compute(h):
        gate_up(ONE, h)
        gate = acc[h, 0]
        hid[0] = (gate * jax.nn.sigmoid(gate) * acc[h, 1]).astype(BF16)

        def step(k, carry):
            part[0, h, :, wide(k)] = jnp.dot(hid[0], held_w[2, :, wide(k)], preferred_element_type=F32).astype(BF16)
            return carry

        lax.fori_loop(0, D // WIDE, step, 0)
        fold(0, h)

    def backward_hidden(h):
        unfold(GRADS, h)
        acc[h, 2] = jnp.zeros((ROWS, HID), F32)

        def down(k, carry):
            acc[h, 2] += lax.dot_general(recv[GRADS, h, :, wide(k)], held_w[2, :, wide(k)], NT, preferred_element_type=F32)
            return carry

        lax.fori_loop(0, D // WIDE, down, 0)
        gate = acc[h, 0]
        sig = jax.nn.sigmoid(gate)
        slope = acc[h, 2] * sig
        hid[0] = (slope * acc[h, 1] * (1.0 + gate * (1.0 - sig))).astype(BF16)
        hid[1] = (slope * gate).astype(BF16)

    def backward_rows(h):
        def step(k, carry):
            total = jnp.dot(hid[0], held_w[0, :, wide(k)], preferred_element_type=F32)
            total = total + jnp.dot(hid[1], held_w[1, :, wide(k)], preferred_element_type=F32)
            part[1, h, :, wide(k)] = total.astype(BF16)
            return carry

        lax.fori_loop(0, D // WIDE, step, 0)
        fold(1, h)

    def to_core(m, half, parity):
        n = half * 2 + parity
        return pltpu.make_async_remote_copy(
            part.at[m, half, pl.ds(pl.multiple_of(place(parity, 1 - c, 0) * BLK, 64), 64)],
            cx.at[m, n],
            xsend.at[m, n],
            xrecv.at[m, n],
            device_id=(p, other),
            device_id_type=MESH,
        )

    def exchange(m, half):
        to_core(m, half, 1 - enters(half)).start()
        to_core(m, half, enters(half)).start()

    def add_into(m, half, b, extra):
        mine = part[m, half, rows16(b), :]
        part[m, half, rows16(b), :] = (mine.astype(F32) + extra.astype(F32)).astype(BF16)

    def to_pair(m, half, source_z):
        n = half * 4 + source_z
        return pltpu.make_async_remote_copy(
            part.at[m, half, rows16(place(1 - enters(half), c, source_z))],
            px.at[m, n],
            psend.at[m, n],
            precv.at[m, n],
            device_id=(p, pair),
            device_id_type=MESH,
        )

    def to_home(m, half, source_z):
        b = place(enters(half), c, source_z)
        target = (x if half == 0 else 3 - x) * 8 + source_z * 2 + c
        src, dst, sem = part.at[m, half, rows16(b)], home.at[m, rows16(expert)], hrecv.at[m, expert]
        return target, src, dst, hsend.at[m, half * 4 + source_z], sem, (p, target)

    def return_first(m, half):
        for parity, leaves in ((1 - enters(half), False), (enters(half), True)):
            n = half * 2 + parity
            pltpu.make_async_copy(cx.at[m, n], cx.at[m, n], xrecv.at[m, n]).wait()

            def step(k, carry):
                source_z = flip(z, 3 - k)
                add_into(m, half, place(parity, c, source_z), cx[m, n, rows16(source_z), :])
                if not leaves:
                    to_pair(m, half, source_z).start()
                return carry

            lax.fori_loop(0, 4, step, 0)

    def return_second(m, half):
        def step(k, carry):
            source_z = flip(z, 3 - k)
            n = half * 4 + source_z
            pltpu.make_async_copy(px.at[m, n], px.at[m, n], precv.at[m, n]).wait()
            add_into(m, half, place(enters(half), c, source_z), px[m, n])
            launch(to_home(m, half, source_z), half == 0)
            return carry

        lax.fori_loop(0, 4, step, 0)

    def drain_dispatch(d):
        def injected(i, carry):
            sent(dispatch(d, i), d == ACTS)
            return carry

        lax.fori_loop(0, EXPERTS, injected, 0)
        for half in range(2):

            def passed(k, carry):
                onward(d, half, place(enters(half), c, k), pair, to_pair_sem(d, half, k)).wait_send()
                for parity in range(2):
                    onward(d, half, place(parity, c, k), other, to_core_sem(d, half, parity, k)).wait_send()
                return carry

            lax.fori_loop(0, 4, passed, 0)

    def drain_return(m):
        for half in range(2):
            to_core(m, half, 0).wait_send()
            to_core(m, half, 1).wait_send()

            def returned(k, carry):
                to_pair(m, half, k).wait_send()
                sent(to_home(m, half, k), half == 0)
                return carry

            lax.fori_loop(0, 4, returned, 0)

    def drain_weights():
        def gone(t, carry):
            pltpu.make_async_remote_copy(
                relay.at[t], relay.at[t], wsend.at[t], wrecv.at[t], device_id=(p, beside), device_id_type=MESH
            ).wait_send()
            return carry

        lax.fori_loop(0, PIECES, gone, 0)

    def result(m, n, out):
        part_of = pl.ds(n * (D // 2), D // 2)
        return pltpu.make_async_copy(held.at[m, :, part_of], out.at[:, part_of], out_sem.at[m, n])

    def collect(m, main_col, tail_col, prob_col, out):
        def step(e, carry):
            pltpu.make_async_copy(home.at[m, rows16(e)], home.at[m, rows16(e)], hrecv.at[m, e]).wait()
            return carry

        lax.fori_loop(0, EXPERTS, step, 0)
        row = iota((TOK, TOK), 1).astype(F32)
        table = onehot(row == main_col)
        tail = home[m, :, D:W]
        for k in range(NK):
            got = jnp.dot(table, home[m, :, k * KB : (k + 1) * KB], preferred_element_type=F32)
            got = got + jnp.dot(onehot(row == tail_col + 2.0 * k), tail, preferred_element_type=F32)
            if prob_col is not None:
                got = prob_col * got
            held[m, :, k * KB : (k + 1) * KB] = got.astype(BF16)
            if k % 4 == 3:
                result(m, k // 4, out).start()

    loads[0].wait()
    fill(ACTS, main_row_two, tail_row_two, None)
    send(ACTS, 0, 8)
    keep_weights()
    loads[1].wait()
    metas[0].wait_recv()
    fill(ONE, meta_in[0, 0:1, :], meta_in[0, 1:2, :], None)
    send(ONE, 0, 8)
    give_all(0)
    give_all(1)
    give_all(2)
    forward(ACTS, 0, True, None, None)
    forward(ACTS, 1, True, None, 0)
    forward(ONE, 0, True, None, 1)
    forward(ONE, 1, True, None, 2)
    loads[2].wait()
    metas[1].wait_recv()
    fill(GRADS, meta_in[1, 0:1, :], meta_in[1, 1:2, :], meta_in[1, 2:3, :])
    send(GRADS, 0, 8)
    forward(ONE, 0, False)
    from_core(ONE, 0)
    forward(ONE, 1, False)
    forward(ACTS, 0, False)
    forward(ACTS, 1, False)
    forward(GRADS, 0, True)
    weights_here()
    forward_compute(0)
    exchange(0, 0)
    forward(GRADS, 1, True)
    from_core(ONE, 1)
    forward_compute(1)
    exchange(0, 1)
    return_first(0, 0)
    return_first(0, 1)
    from_core(ACTS, 0)
    forward(GRADS, 0, False)
    gate_up(ACTS, 0)
    from_core(ACTS, 1)
    forward(GRADS, 1, False)
    gate_up(ACTS, 1)
    from_core(GRADS, 0)
    backward_hidden(0)
    backward_rows(0)
    exchange(1, 0)
    return_second(0, 0)
    from_core(GRADS, 1)
    backward_hidden(1)
    return_first(1, 0)
    backward_rows(1)
    exchange(1, 1)
    return_second(0, 1)
    return_first(1, 1)
    return_second(1, 0)
    drain_dispatch(ACTS)
    drain_dispatch(ONE)
    drain_dispatch(GRADS)
    drain_weights()
    for copy in metas:
        copy.wait_send()
    return_second(1, 1)
    drain_return(0)
    collect(0, main_col_one, tail_col_one, column(probs_one[...]), out_one)
    collect(1, main_col_two, tail_col_two, None, out_two)
    drain_return(1)
    for n in range(2):
        result(0, n, out_one).wait()
        result(1, n, out_two).wait()


def body(
    first_acts,
    first_routes,
    first_probs,
    second_acts,
    second_grads,
    second_routes,
    second_probs,
    gate_weight,
    up_weight,
    down_weight,
):
    vmem = pl.BlockSpec(memory_space=pltpu.VMEM)
    hbm = pl.BlockSpec(memory_space=pl.ANY)
    dma = pltpu.SemaphoreType.DMA
    result = jax.ShapeDtypeStruct((TOK, D), BF16)
    first_out, input_grads = pl.pallas_call(
        kernel,
        out_shape=(result, result),
        in_specs=[vmem] * 4 + [hbm] * 6,
        out_specs=(hbm, hbm),
        scratch_shapes=[
            pltpu.VMEM((3, TOK, D), BF16),
            pltpu.VMEM((3, HID, D), BF16),
            pltpu.VMEM((2, 8, TOK), F32),
            pltpu.VMEM((2, 8, TOK), F32),
            pltpu.VMEM((3, EXPERTS * BLK, W), BF16),
            pltpu.VMEM((3, 2, ROWS, W), BF16),
            pltpu.VMEM((2, 2, ROWS, W), BF16),
            pltpu.VMEM((2, 4, 4 * BLK, W), BF16),
            pltpu.VMEM((2, 8, BLK, W), BF16),
            pltpu.VMEM((2, EXPERTS * BLK, W), BF16),
            pltpu.VMEM((2, 3, ROWS, HID), F32),
            pltpu.VMEM((2, ROWS, HID), BF16),
            pltpu.VMEM((PIECES, PIECE, D), BF16),
            dma((3,)),
            dma((2,)),
            dma((2,)),
            dma((3, EXPERTS)),
            dma((3, 8)),
            dma((3, 16)),
            dma((3, SRC)),
            dma((2, 4)),
            dma((2, 4)),
            dma((2, 8)),
            dma((2, 8)),
            dma((2, 8)),
            dma((2, EXPERTS)),
            dma((PIECES,)),
            dma((PIECES,)),
            dma((PIECES,)),
            dma((2, 2)),
        ],
        compiler_params=pltpu.CompilerParams(
            collective_id=0, has_side_effects=True, vmem_limit_bytes=63 * 1024 * 1024
        ),
    )(
        first_routes.reshape(1, TOK),
        first_probs.reshape(1, TOK),
        second_routes.reshape(1, TOK),
        second_probs.reshape(1, TOK),
        first_acts[0],
        second_acts[0],
        second_grads[0],
        gate_weight[0].T,
        up_weight[0].T,
        down_weight[0],
    )
    return (first_out[None], input_grads[None])


def solution(mesh):
    in_specs = (
        P("pipe", "ep", None),
        P("pipe", "ep", None),
        P("pipe", "ep", None),
        P("pipe", "ep", None),
        P("pipe", "ep", None),
        P("pipe", "ep", None),
        P("pipe", "ep", None),
        P("pipe", None, "ep"),
        P("pipe", None, "ep"),
        P("pipe", "ep", None),
    )
    out_specs = (P("pipe", "ep", None), P("pipe", "ep", None))
    return jax.shard_map(body, mesh=mesh, in_specs=in_specs, out_specs=out_specs, check_vma=False)
```

```python
import jax
import jax.numpy as jnp
from jax import lax
from jax.experimental import pallas as pl
from jax.experimental.pallas import tpu as pltpu
from jax.sharding import PartitionSpec as P

MESH = pl.DeviceIdType.MESH
F32 = jnp.float32
BF16 = jnp.bfloat16
NT = (((1,), (1,)), ((), ()))

TOK = 128
D = 4096
HID = 192
EXPERTS = 8
KB = 512
NK = D // KB
WIDE = 1024
W = D + KB
BLK = 16
SRC = 32
SPLIT = 4
PIECE = HID // SPLIT
PIECES = 3 * SPLIT
HALF = SRC // 2
MAIN = HALF * BLK
EXTRA = HALF * 2
ROWS = MAIN + EXTRA
SECTIONS = 8

ONE, ACTS, GRADS = 0, 1, 2


def rows16(index):
    return pl.ds(pl.multiple_of(index * BLK, BLK), BLK)


def cols(index):
    return pl.ds(pl.multiple_of(index * KB, KB), KB)


def wide(index):
    return pl.ds(pl.multiple_of(index * WIDE, WIDE), WIDE)


def iota(shape, dim):
    return lax.broadcasted_iota(jnp.int32, shape, dim)


def onehot(mask):
    return jnp.where(mask, 1.0, 0.0).astype(BF16)


def column(row):
    eye = iota((TOK, TOK), 0) == iota((TOK, TOK), 1)
    return jnp.sum(jnp.where(eye, jnp.broadcast_to(row, (TOK, TOK)), 0.0), axis=1, keepdims=True)


def codes(expert_row):
    here, there = iota((TOK, TOK), 0), iota((TOK, TOK), 1)
    row = expert_row.astype(F32)
    col = column(row)
    same = jnp.where(col == row, 1.0, 0.0)
    slot_col = jnp.sum(jnp.where(there < here, same, 0.0), axis=1, keepdims=True)
    slot_row = jnp.sum(jnp.where(here < there, same, 0.0), axis=0, keepdims=True)

    def both(expert, slot):
        main = jnp.where(slot < BLK, expert * BLK + slot, -1.0)
        tail = jnp.where(slot < BLK, -1024.0, expert * BLK + slot - BLK)
        return main, tail

    return both(col, slot_col), both(row, slot_row)


def flip(z, k):
    return (z % 2 + k % 2) % 2 + 2 * ((z // 2 + k // 2) % 2)


def kernel(
    routes_one, probs_one, routes_two, probs_two, one_hbm, acts_hbm, grads_hbm, gate_hbm, up_hbm, down_hbm,
    out,
    held, held_w, meta_out, meta_in, stage, recv, part, cx, px, home, acc, hid, relay,
    load_sem, msend, mrecv, dsend, fsend, csend, rsem, xsend, xrecv, psend, precv, hsend, hrecv,
    wsend, wrecv, relay_recv, out_sem,
):
    p, j = lax.axis_index("pipe"), lax.axis_index("ep")
    x, z, c = j // 8, (j // 2) % 4, j % 2
    columns = x // 2
    flipped_x, flipped_z = flip(x, 1), flip(z, 1)
    expert = (columns * 2 + z % 2) * 2 + z // 2
    other = x * 8 + z * 2 + (1 - c)
    pair = flipped_x * 8 + z * 2 + c
    even = x % 2 == z % 2
    relays = jnp.logical_and(c == 1, even)
    round_x, round_z = jnp.where(even, flipped_x, x), jnp.where(even, z, flipped_z)
    beside = flipped_x * 8 + z * 2 + 1
    beyond = x * 8 + flipped_z * 2 + 1
    after, before = lax.rem(p + 1, SECTIONS), lax.rem(p + SECTIONS - 1, SECTIONS)
    section = {ONE: after, ACTS: p, GRADS: before}

    loads = [
        pltpu.make_async_copy(src, held.at[d], load_sem.at[d])
        for d, src in ((ACTS, acts_hbm), (ONE, one_hbm), (GRADS, grads_hbm))
    ]
    for load in loads:
        load.start()

    weights = (gate_hbm, up_hbm, down_hbm)

    def slot(i, n):
        return held_w.at[i, pl.ds(n * PIECE, PIECE)]

    def keep_weights():
        for i in range(3):
            for n in range(SPLIT):
                src = weights[i].at[pl.ds(n * PIECE, PIECE)]
                pl.when(relays)(pltpu.make_async_copy(src, slot(i, n), wrecv.at[i * SPLIT + n]).start)

    def give_weight(i, n):
        part_of, t = pl.ds(pl.multiple_of(n * PIECE, BLK), PIECE), i * SPLIT + n
        src = weights[i].at[part_of]

        @pl.when(c == 0)
        def _():
            pltpu.make_async_remote_copy(
                src, held_w.at[i, part_of], wsend.at[0], wrecv.at[t],
                device_id=(p, round_x * 8 + round_z * 2), device_id_type=MESH,
            ).start()

        @pl.when(jnp.logical_and(c == 1, jnp.logical_not(even)))
        def _():
            pltpu.make_async_remote_copy(
                src, relay.at[t], wsend.at[0], relay_recv.at[t], device_id=(p, beside), device_id_type=MESH
            ).start()

    def give_all(i):
        def step(n, carry):
            give_weight(i, n)
            return carry

        lax.fori_loop(0, SPLIT, step, 0)

    def relay_weight(t):
        @pl.when(relays)
        def _():
            pltpu.make_async_copy(relay.at[t], relay.at[t], relay_recv.at[t]).wait()
            pltpu.make_async_remote_copy(
                relay.at[t],
                held_w.at[t // SPLIT, pl.ds(pl.multiple_of((t % SPLIT) * PIECE, BLK), PIECE)],
                wsend.at[0],
                wrecv.at[t],
                device_id=(p, beyond),
                device_id_type=MESH,
            ).start()

    def weights_here():
        for i in range(3):
            for n in range(SPLIT):
                pltpu.make_async_copy(slot(i, n), slot(i, n), wrecv.at[i * SPLIT + n]).wait()

    barrier = pltpu.get_barrier_semaphore()

    def greet(n, carry):
        them = (n // 4) * 8 + (n % 4) * 2 + c
        pl.semaphore_signal(barrier, inc=1, device_id=(after, them), device_id_type=MESH)
        pl.semaphore_signal(barrier, inc=1, device_id=(before, them), device_id_type=MESH)

        @pl.when(them != j)
        def _():
            pl.semaphore_signal(barrier, inc=1, device_id=(p, them), device_id_type=MESH)

        return carry

    lax.fori_loop(0, 16, greet, 0)
    pl.semaphore_signal(barrier, inc=1, device_id=(p, other), device_id_type=MESH)

    (main_col_one, tail_col_one), (main_row_one, tail_row_one) = codes(routes_one[...])
    (main_col_two, tail_col_two), (main_row_two, tail_row_two) = codes(routes_two[...])
    meta_out[0, 0:1, :] = main_row_one
    meta_out[0, 1:2, :] = tail_row_one
    meta_out[0, 2:8, :] = jnp.zeros((6, TOK), F32)
    meta_out[1, 0:1, :] = main_row_two
    meta_out[1, 1:2, :] = tail_row_two
    meta_out[1, 2:3, :] = probs_two[...]
    meta_out[1, 3:8, :] = jnp.zeros((5, TOK), F32)

    pl.semaphore_wait(barrier, 48)

    metas = [
        pltpu.make_async_remote_copy(
            meta_out.at[i], meta_in.at[i], msend.at[i], mrecv.at[i], device_id=(to, j), device_id_type=MESH
        )
        for i, to in enumerate((before, after))
    ]
    for copy in metas:
        copy.start()

    def fill(d, main_row, tail_row, prob_row):
        row = iota((TOK, TOK), 0).astype(F32)
        here = row == main_row
        table = onehot(here)
        tail = jnp.zeros((TOK, KB), F32)
        tail_prob = jnp.zeros((TOK, 1), F32)
        if prob_row is not None:
            prob = jnp.sum(jnp.where(here, prob_row, 0.0), axis=1, keepdims=True)
        for k in range(NK):
            values = held[d, :, k * KB : (k + 1) * KB]
            got = jnp.dot(table, values, preferred_element_type=F32)
            there = row == tail_row + 2.0 * k
            tail = tail + jnp.dot(onehot(there), values, preferred_element_type=F32)
            if prob_row is not None:
                got = prob * got
                tail_prob = tail_prob + jnp.sum(jnp.where(there, prob_row, 0.0), axis=1, keepdims=True)
            stage[d, :, k * KB : (k + 1) * KB] = got.astype(BF16)
        if prob_row is not None:
            tail = tail_prob * tail
        stage[d, :, D:W] = tail.astype(BF16)

    def place(parity, core, source_z):
        return parity * 8 + core * 4 + source_z

    def enters(half):
        return (x + half) % 2

    def launch(move, may_stay):
        target, src, dst, send_sem, sem, device = move

        def remote():
            pltpu.make_async_remote_copy(src, dst, send_sem, sem, device_id=device, device_id_type=MESH).start()

        if not may_stay:
            remote()
            return
        pl.when(target != j)(remote)

        @pl.when(target == j)
        def _():
            pltpu.make_async_copy(src, dst, sem).start()

    def dispatch(d, i):
        half = i // 4
        to_z = flip(z, i % 4 if d == ACTS else 3 - i % 4)
        to_columns = jnp.where(half == 0, columns, 1 - columns)
        target = jnp.where(half == 0, x, 3 - x) * 8 + to_z * 2 + c
        e = (to_columns * 2 + to_z % 2) * 2 + to_z // 2
        b = place(x % 2, c, z)
        sem = rsem.at[d, half * HALF + b]
        src, dst = stage.at[d, rows16(e)], recv.at[d, half, rows16(b)]
        return target, src, dst, dsend.at[d], sem, (section[d], target)

    def send(d, low, high):
        def step(i, carry):
            launch(dispatch(d, i), d == ACTS)
            return carry

        lax.fori_loop(low, high, step, 0)

    def arrived(d, h, b):
        ref = recv.at[d, h, rows16(b)]
        pltpu.make_async_copy(ref, ref, rsem.at[d, h * HALF + b]).wait()

    def onward(d, half, b, to, sem):
        ref = recv.at[d, half, rows16(b)]
        return pltpu.make_async_remote_copy(
            ref, ref, sem, rsem.at[d, half * HALF + b], device_id=(p, to), device_id_type=MESH
        )

    def to_pair_sem(d, half, source_z):
        return fsend.at[d]

    def to_core_sem(d, half, parity, source_z):
        return csend.at[d]

    def forward(d, half, direct, give=None, relay_of=None):
        parity = enters(half) if direct else 1 - enters(half)

        def step(k, carry):
            source_z = flip(z, k if d == ACTS else 3 - k)
            b = place(parity, c, source_z)
            arrived(d, half, b)
            if direct:
                onward(d, half, b, pair, to_pair_sem(d, half, source_z)).start()
            onward(d, half, b, other, to_core_sem(d, half, parity, source_z)).start()
            if give is not None:
                give_weight(give, k)
            if relay_of is not None:
                relay_weight(relay_of * SPLIT + k)
            return carry

        lax.fori_loop(0, 4, step, 0)

    def from_core(d, half):
        def step(k, carry):
            arrived(d, half, place(k // 4, 1 - c, k % 4))
            return carry

        lax.fori_loop(0, 8, step, 0)

    def unfold(d, h):
        row, col = iota((EXTRA, MAIN), 0), iota((EXTRA, MAIN), 1)
        base = (row // 2) * BLK + row % 2
        tail = recv[d, h, 0:MAIN, D:W]
        for k in range(NK):
            pick = onehot(col == base + 2 * k)
            recv[d, h, MAIN:ROWS, k * KB : (k + 1) * KB] = jnp.dot(pick, tail, preferred_element_type=F32).astype(BF16)

    def fold(m, h):
        row, col = iota((MAIN, EXTRA), 0), iota((MAIN, EXTRA), 1)
        base = (col // 2) * BLK + col % 2
        tail = jnp.zeros((MAIN, KB), F32)
        for k in range(NK):
            pick = onehot(row == base + 2 * k)
            tail = tail + jnp.dot(pick, part[m, h, MAIN:ROWS, k * KB : (k + 1) * KB], preferred_element_type=F32)
        part[m, h, 0:MAIN, D:W] = tail.astype(BF16)

    def gate_up(d, h):
        unfold(d, h)
        acc[h, 0:2] = jnp.zeros((2, ROWS, HID), F32)

        def step(k, carry):
            values = recv[d, h, :, wide(k)]
            acc[h, 0] += lax.dot_general(values, held_w[0, :, wide(k)], NT, preferred_element_type=F32)
            acc[h, 1] += lax.dot_general(values, held_w[1, :, wide(k)], NT, preferred_element_type=F32)
            return carry

        lax.fori_loop(0, D // WIDE, step, 0)

    def forward_compute(h):
        gate_up(ONE, h)
        gate = acc[h, 0]
        hid[0] = (gate * jax.nn.sigmoid(gate) * acc[h, 1]).astype(BF16)

        def step(k, carry):
            part[0, h, :, wide(k)] = jnp.dot(hid[0], held_w[2, :, wide(k)], preferred_element_type=F32).astype(BF16)
            return carry

        lax.fori_loop(0, D // WIDE, step, 0)
        fold(0, h)

    def backward_hidden(h):
        unfold(GRADS, h)
        acc[h, 2] = jnp.zeros((ROWS, HID), F32)

        def down(k, carry):
            acc[h, 2] += lax.dot_general(recv[GRADS, h, :, wide(k)], held_w[2, :, wide(k)], NT, preferred_element_type=F32)
            return carry

        lax.fori_loop(0, D // WIDE, down, 0)
        gate = acc[h, 0]
        sig = jax.nn.sigmoid(gate)
        slope = acc[h, 2] * sig
        hid[0] = (slope * acc[h, 1] * (1.0 + gate * (1.0 - sig))).astype(BF16)
        hid[1] = (slope * gate).astype(BF16)

    def backward_rows(h):
        def step(k, carry):
            total = jnp.dot(hid[0], held_w[0, :, wide(k)], preferred_element_type=F32)
            total = total + jnp.dot(hid[1], held_w[1, :, wide(k)], preferred_element_type=F32)
            part[1, h, :, wide(k)] = total.astype(BF16)
            return carry

        lax.fori_loop(0, D // WIDE, step, 0)
        fold(1, h)

    def to_core(m, half, parity):
        n = half * 2 + parity
        return pltpu.make_async_remote_copy(
            part.at[m, half, pl.ds(pl.multiple_of(place(parity, 1 - c, 0) * BLK, 64), 64)],
            cx.at[m, n],
            xsend.at[m, n],
            xrecv.at[m, n],
            device_id=(p, other),
            device_id_type=MESH,
        )

    def exchange(m, half):
        to_core(m, half, 1 - enters(half)).start()
        to_core(m, half, enters(half)).start()

    def add_into(m, half, b, extra):
        mine = part[m, half, rows16(b), :]
        part[m, half, rows16(b), :] = (mine.astype(F32) + extra.astype(F32)).astype(BF16)

    def to_pair(m, half, source_z):
        n = half * 4 + source_z
        return pltpu.make_async_remote_copy(
            part.at[m, half, rows16(place(1 - enters(half), c, source_z))],
            px.at[m, n],
            psend.at[m],
            precv.at[m, n],
            device_id=(p, pair),
            device_id_type=MESH,
        )

    def to_home(m, half, source_z):
        b = place(enters(half), c, source_z)
        target = (x if half == 0 else 3 - x) * 8 + source_z * 2 + c
        src, dst, sem = part.at[m, half, rows16(b)], home.at[m, rows16(expert)], hrecv.at[m, expert]
        return target, src, dst, hsend.at[m], sem, (p, target)

    def return_first(m, half):
        for parity, leaves in ((1 - enters(half), False), (enters(half), True)):
            n = half * 2 + parity
            pltpu.make_async_copy(cx.at[m, n], cx.at[m, n], xrecv.at[m, n]).wait()

            def step(k, carry):
                source_z = flip(z, 3 - k)
                add_into(m, half, place(parity, c, source_z), cx[m, n, rows16(source_z), :])
                if not leaves:
                    to_pair(m, half, source_z).start()
                return carry

            lax.fori_loop(0, 4, step, 0)

    def return_second(m, half):
        def step(k, carry):
            source_z = flip(z, 3 - k)
            n = half * 4 + source_z
            pltpu.make_async_copy(px.at[m, n], px.at[m, n], precv.at[m, n]).wait()
            add_into(m, half, place(enters(half), c, source_z), px[m, n])
            launch(to_home(m, half, source_z), half == 0)
            return carry

        lax.fori_loop(0, 4, step, 0)

    def all_sent(ref, sem):
        pltpu.make_async_remote_copy(ref, ref, sem, sem, device_id=(p, other), device_id_type=MESH).wait_send()

    def drain_dispatch(d):
        all_sent(stage.at[d, pl.ds(0, (7 if d == ACTS else 8) * BLK)], dsend.at[d])
        all_sent(recv.at[d, 0, pl.ds(0, 8 * BLK)], fsend.at[d])
        all_sent(recv.at[d, 0, pl.ds(0, 16 * BLK)], csend.at[d])

    def drain_return(m):
        for half in range(2):
            to_core(m, half, 0).wait_send()
            to_core(m, half, 1).wait_send()
        all_sent(part.at[m, 0, pl.ds(0, 8 * BLK)], psend.at[m])
        all_sent(part.at[m, 0, pl.ds(0, 7 * BLK)], hsend.at[m])

    def drain_weights():
        all_sent(relay, wsend.at[0])

    def result(m, n):
        part_of = pl.ds(n * (D // 2), D // 2)
        return pltpu.make_async_copy(held.at[m, :, part_of], out.at[m, :, part_of], out_sem.at[m, n])

    def collect(m, main_col, tail_col, prob_col):
        def step(e, carry):
            pltpu.make_async_copy(home.at[m, rows16(e)], home.at[m, rows16(e)], hrecv.at[m, e]).wait()
            return carry

        lax.fori_loop(0, EXPERTS, step, 0)
        row = iota((TOK, TOK), 1).astype(F32)
        table = onehot(row == main_col)
        tail = home[m, :, D:W]
        for k in range(NK):
            got = jnp.dot(table, home[m, :, k * KB : (k + 1) * KB], preferred_element_type=F32)
            got = got + jnp.dot(onehot(row == tail_col + 2.0 * k), tail, preferred_element_type=F32)
            if prob_col is not None:
                got = prob_col * got
            held[m, :, k * KB : (k + 1) * KB] = got.astype(BF16)
            if k % 4 == 3:
                result(m, k // 4).start()

    loads[0].wait()
    fill(ACTS, main_row_two, tail_row_two, None)
    send(ACTS, 0, 8)
    keep_weights()
    loads[1].wait()
    metas[0].wait_recv()
    fill(ONE, meta_in[0, 0:1, :], meta_in[0, 1:2, :], None)
    send(ONE, 0, 8)
    give_all(0)
    give_all(1)
    give_all(2)
    forward(ACTS, 0, True, None, None)
    forward(ACTS, 1, True, None, 0)
    forward(ONE, 0, True, None, 1)
    forward(ONE, 1, True, None, 2)
    loads[2].wait()
    metas[1].wait_recv()
    fill(GRADS, meta_in[1, 0:1, :], meta_in[1, 1:2, :], meta_in[1, 2:3, :])
    send(GRADS, 0, 8)
    forward(ONE, 0, False)
    from_core(ONE, 0)
    forward(ONE, 1, False)
    forward(ACTS, 0, False)
    forward(ACTS, 1, False)
    forward(GRADS, 0, True)
    weights_here()
    forward_compute(0)
    exchange(0, 0)
    forward(GRADS, 1, True)
    from_core(ONE, 1)
    forward_compute(1)
    exchange(0, 1)
    return_first(0, 0)
    return_first(0, 1)
    from_core(ACTS, 0)
    forward(GRADS, 0, False)
    gate_up(ACTS, 0)
    from_core(ACTS, 1)
    forward(GRADS, 1, False)
    gate_up(ACTS, 1)
    from_core(GRADS, 0)
    backward_hidden(0)
    backward_rows(0)
    exchange(1, 0)
    return_second(0, 0)
    from_core(GRADS, 1)
    backward_hidden(1)
    return_first(1, 0)
    backward_rows(1)
    exchange(1, 1)
    return_second(0, 1)
    return_first(1, 1)
    return_second(1, 0)
    drain_dispatch(ACTS)
    drain_dispatch(ONE)
    drain_dispatch(GRADS)
    drain_weights()
    for copy in metas:
        copy.wait_send()
    return_second(1, 1)
    drain_return(0)
    collect(0, main_col_one, tail_col_one, column(probs_one[...]))
    collect(1, main_col_two, tail_col_two, None)
    drain_return(1)
    for n in range(2):
        result(0, n).wait()
        result(1, n).wait()


def body(
    first_acts,
    first_routes,
    first_probs,
    second_acts,
    second_grads,
    second_routes,
    second_probs,
    gate_weight,
    up_weight,
    down_weight,
):
    vmem = pl.BlockSpec(memory_space=pltpu.VMEM)
    hbm = pl.BlockSpec(memory_space=pl.ANY)
    dma = pltpu.SemaphoreType.DMA
    both = pl.pallas_call(
        kernel,
        out_shape=jax.ShapeDtypeStruct((2, TOK, D), BF16),
        in_specs=[vmem] * 4 + [hbm] * 6,
        out_specs=hbm,
        scratch_shapes=[
            pltpu.VMEM((3, TOK, D), BF16),
            pltpu.VMEM((3, HID, D), BF16),
            pltpu.VMEM((2, 8, TOK), F32),
            pltpu.VMEM((2, 8, TOK), F32),
            pltpu.VMEM((3, EXPERTS * BLK, W), BF16),
            pltpu.VMEM((3, 2, ROWS, W), BF16),
            pltpu.VMEM((2, 2, ROWS, W), BF16),
            pltpu.VMEM((2, 4, 4 * BLK, W), BF16),
            pltpu.VMEM((2, 8, BLK, W), BF16),
            pltpu.VMEM((2, EXPERTS * BLK, W), BF16),
            pltpu.VMEM((2, 3, ROWS, HID), F32),
            pltpu.VMEM((2, ROWS, HID), BF16),
            pltpu.VMEM((PIECES, PIECE, D), BF16),
            dma((3,)),
            dma((2,)),
            dma((2,)),
            dma((3,)),
            dma((3,)),
            dma((3,)),
            dma((3, SRC)),
            dma((2, 4)),
            dma((2, 4)),
            dma((2,)),
            dma((2, 8)),
            dma((2,)),
            dma((2, EXPERTS)),
            dma((1,)),
            dma((PIECES,)),
            dma((PIECES,)),
            dma((2, 2)),
        ],
        compiler_params=pltpu.CompilerParams(
            collective_id=0, has_side_effects=True, vmem_limit_bytes=63 * 1024 * 1024
        ),
    )(
        first_routes.reshape(1, TOK),
        first_probs.reshape(1, TOK),
        second_routes.reshape(1, TOK),
        second_probs.reshape(1, TOK),
        first_acts[0],
        second_acts[0],
        second_grads[0],
        gate_weight[0].T,
        up_weight[0].T,
        down_weight[0],
    )
    return (both[0:1], both[1:2])


def solution(mesh):
    in_specs = (
        P("pipe", "ep", None),
        P("pipe", "ep", None),
        P("pipe", "ep", None),
        P("pipe", "ep", None),
        P("pipe", "ep", None),
        P("pipe", "ep", None),
        P("pipe", "ep", None),
        P("pipe", None, "ep"),
        P("pipe", None, "ep"),
        P("pipe", "ep", None),
    )
    out_specs = (P("pipe", "ep", None), P("pipe", "ep", None))
    return jax.shard_map(body, mesh=mesh, in_specs=in_specs, out_specs=out_specs, check_vma=False)
```
